256 devices in a mesh: img: 8 (over y_lo, x), txt: 32 (over z, y_hi, core).
Axes of the slice: x: 4, y: 4 (y_hi: 2, y_lo: 2; y = y_hi * 2 + y_lo), z: 8, core: 2. Of those that a mesh axis runs over, the one named last changes fastest.
Arguments:
- feats: bfloat16 [1024, 257, 1408], P(('img', 'txt')), may hold values from -12 to 12
- query_states: bfloat16 [32, 768], replicated, may hold values from -6 to 6
- w_query: bfloat16 [768, 768], replicated, may hold values from -0.21875 to 0.21875
- w_key: bfloat16 [1408, 768], replicated, may hold values from -0.15625 to 0.15625
- w_value: bfloat16 [1408, 768], replicated, may hold values from -1 to 1
- w_out: bfloat16 [768, 768], replicated, may hold values from -1 to 1
- ln_gain: float32 [768], replicated, may hold values from 0.25 to 1.75
- w_proj: bfloat16 [768, 256], replicated, may hold values from -1 to 1
- text_feats: bfloat16 [1024, 256], P('txt'), may hold values from -8 to 8
- i2t_index: int32 [1024], replicated, may hold values from 0 to 31
- t2i_index: int32 [1024], replicated, may hold values from 0 to 31
Outputs:
- query_grad: bfloat16 [1024, 32, 768], P(('img', 'txt'))
- row_loss: float32 [1024], P(('img', 'txt'))
- col_loss: float32 [1024], P('txt')
The draws below stay inside these ranges and needn't reach their ends.
All inputs are finite; a program needn't handle non-finite values.
Results may differ from the reference program's by a relative error of at most 0.022.
Values may be sent and summed in bfloat16 or wider, within the bound.
No kernel may reach another device: no remote copies, remote signals or barrier semaphores. Data moves between devices by JAX's collectives and lax.ppermute only.
A program may use at most 64 MiB of HBM per device.

```python
import math
import jax
import jax.numpy as jnp
from jax import lax

FEAT = 1408
PATCHES = 257
HIDDEN_SIZE = 768
HEADS = 12
HEAD = 64
QUERIES = 32
EMBED = 256
IMG_DEV = 4
PAIRS = 1024
N_IMG = 8
N_TXT = 32


def query_base(key):
    return jnp.clip(jax.random.normal(jax.random.fold_in(key, 101), (QUERIES, HIDDEN_SIZE), jnp.float32), -6.0, 6.0)


def value_base(key):
    return jnp.clip(jax.random.normal(jax.random.fold_in(key, 102), (FEAT, HIDDEN_SIZE), jnp.float32) / math.sqrt(FEAT), -1.0, 1.0)


def output_base(key):
    return jnp.clip(jax.random.normal(jax.random.fold_in(key, 103), (HIDDEN_SIZE, HIDDEN_SIZE), jnp.float32) / math.sqrt(HIDDEN_SIZE), -1.0, 1.0)


def embed_base(key):
    return jnp.clip(jax.random.normal(jax.random.fold_in(key, 104), (HIDDEN_SIZE, EMBED), jnp.float32) / math.sqrt(HIDDEN_SIZE), -1.0, 1.0)


def chosen_base(key):
    return jax.random.randint(jax.random.fold_in(key, 105), (PAIRS,), 0, QUERIES, dtype=jnp.int32)


def image_means(key, lowest, highest):
    scales = jnp.exp(jax.random.uniform(jax.random.fold_in(key, 106), (PAIRS, 1), jnp.float32, math.log(lowest), math.log(highest)))
    return scales * jnp.clip(jax.random.normal(jax.random.fold_in(key, 107), (PAIRS, FEAT), jnp.float32), -4.0, 4.0)


def draw_query_states(key, part):
    return query_base(key).astype(jnp.bfloat16)


def draw_w_value(key, part):
    return value_base(key).astype(jnp.bfloat16)


def draw_w_out(key, part):
    return output_base(key).astype(jnp.bfloat16)


def draw_w_proj(key, part):
    return embed_base(key).astype(jnp.bfloat16)


def draw_t2i_index(key, part):
    return chosen_base(key)


def draw_feats(key, part):
    means = image_means(key, 0.8, 2.0)
    key = jax.random.fold_in(key, 11)
    noise = jnp.clip(jax.random.normal(key, (PAIRS, PATCHES, FEAT), jnp.float32), -6.0, 6.0)
    return jnp.clip(means[:, None, :] + noise, -12.0, 12.0).astype(jnp.bfloat16)


def text_directions(key, lowest, highest):
    states = query_base(key)
    chosen = chosen_base(key)
    means = image_means(key, lowest, highest)
    image_part = jnp.dot(jnp.dot(means, value_base(key), precision=lax.Precision.HIGHEST), output_base(key), precision=lax.Precision.HIGHEST)
    mixed = states[chosen] + image_part
    centered = mixed - jnp.mean(mixed, axis=-1, keepdims=True)
    normed = centered * lax.rsqrt(jnp.mean(centered * centered, axis=-1, keepdims=True) + 1e-06)
    projected = jnp.dot(normed, embed_base(key), precision=lax.Precision.HIGHEST)
    return projected * lax.rsqrt(jnp.sum(projected * projected, axis=-1, keepdims=True) + 1e-06) * math.sqrt(EMBED)


def draw_text_feats(key, part):
    direction = text_directions(key, 0.8, 2.0)
    key = jax.random.fold_in(key, 12)
    noise = jnp.clip(jax.random.normal(key, (PAIRS, EMBED), jnp.float32), -4.0, 4.0)
    amount = 2.0
    return jnp.clip(amount * direction + noise, -8.0, 8.0).astype(jnp.bfloat16)


def set_ends(drawn, rng, least, high):
    extent = drawn.shape
    index_at = [jax.random.randint(jax.random.fold_in(rng, axis), (), 0, extent[axis]) for axis in range(len(extent))]
    drawn = drawn.at[tuple(index_at)].set(least)
    longest = extent.index(max(extent))
    index_at[longest] = (index_at[longest] + 1) % extent[longest]
    return drawn.at[tuple(index_at)].set(high)


def scatter_about(own_key, shape, scale, bound, held_as=jnp.bfloat16):
    values = scale * jax.random.normal(own_key, shape, jnp.float32)
    return jnp.clip(values, min=-bound, max=bound).astype(held_as)


def setup_inputs(seed: int = 0) -> dict:
    arg_keys = jax.random.split(jax.random.key(seed), 12)
    feats = draw_feats(jax.random.fold_in(arg_keys[11], 71), 0)
    query_states = draw_query_states(jax.random.fold_in(arg_keys[11], 71), 0)
    w_query = scatter_about(arg_keys[2], (HIDDEN_SIZE, HIDDEN_SIZE), HIDDEN_SIZE ** -0.5, 0.21875)
    w_key = scatter_about(arg_keys[3], (FEAT, HIDDEN_SIZE), FEAT ** -0.5, 0.15625)
    w_value = draw_w_value(jax.random.fold_in(arg_keys[11], 71), 0)
    w_out = draw_w_out(jax.random.fold_in(arg_keys[11], 71), 0)
    ln_gain = jnp.clip(1.0 + 0.15 * jax.random.normal(arg_keys[6], (HIDDEN_SIZE,), jnp.float32), 0.25, 1.75)
    w_proj = draw_w_proj(jax.random.fold_in(arg_keys[11], 71), 0)
    text_feats = draw_text_feats(jax.random.fold_in(arg_keys[11], 71), 0)
    i2t_index = set_ends(jax.random.randint(arg_keys[9], (PAIRS,), 0, QUERIES), jax.random.fold_in(arg_keys[9], 1), 0, QUERIES - 1).astype(jnp.int32)
    t2i_index = draw_t2i_index(jax.random.fold_in(arg_keys[11], 71), 0)
    return {"feats": feats, "query_states": query_states, "w_query": w_query, "w_key": w_key, "w_value": w_value, "w_out": w_out, "ln_gain": ln_gain, "w_proj": w_proj, "text_feats": text_feats, "i2t_index": i2t_index, "t2i_index": t2i_index}


LOGIT_SCALE = 1.0 / 0.07

def encode(feats, query_states, w_query, w_key, w_value, w_out, ln_gain, w_proj):
    count = feats.shape[0]
    qhead = jnp.dot(query_states, w_query, preferred_element_type=jnp.float32).astype(jnp.bfloat16)
    flat = feats.reshape(count * PATCHES, FEAT)
    keys = jnp.dot(flat, w_key, preferred_element_type=jnp.float32).astype(jnp.bfloat16)
    values = jnp.dot(flat, w_value, preferred_element_type=jnp.float32).astype(jnp.bfloat16)
    keys = keys.reshape(count, PATCHES, HEADS, HEAD).astype(jnp.float32)
    values = values.reshape(count, PATCHES, HEADS, HEAD).astype(jnp.float32)
    qfour = qhead.reshape(QUERIES, HEADS, HEAD).astype(jnp.float32)
    scores = jnp.einsum('qhd,bshd->bhqs', qfour, keys) / math.sqrt(HEAD)
    scores = scores - lax.optimization_barrier(jnp.max(scores, axis=-1, keepdims=True))
    expo = jnp.exp(scores)
    probs = (expo / lax.optimization_barrier(jnp.sum(expo, axis=-1, keepdims=True))).astype(jnp.bfloat16)
    attended = jnp.einsum('bhqs,bshd->bqhd', probs.astype(jnp.float32), values).astype(jnp.bfloat16)
    attended = attended.reshape(count * QUERIES, HIDDEN_SIZE)
    mixed = query_states.astype(jnp.float32)[None] + jnp.dot(attended, w_out, preferred_element_type=jnp.float32).reshape(count, QUERIES, HIDDEN_SIZE)
    centered = mixed - lax.optimization_barrier(jnp.mean(mixed, axis=-1, keepdims=True))
    variance = lax.optimization_barrier(jnp.mean(centered * centered, axis=-1, keepdims=True))
    q_out = centered * lax.rsqrt(variance + 1e-06) * ln_gain
    q_low = q_out.astype(jnp.bfloat16).reshape(count * QUERIES, HIDDEN_SIZE)
    proj = jnp.dot(q_low, w_proj, preferred_element_type=jnp.float32).reshape(count, QUERIES, EMBED)
    inverse = lax.rsqrt(lax.optimization_barrier(jnp.sum(proj * proj, axis=-1, keepdims=True)) + 1e-06)
    unit = proj * inverse
    return (unit.astype(jnp.bfloat16), unit, inverse)

def reference(feats, query_states, w_query, w_key, w_value, w_out, ln_gain, w_proj, text_feats, i2t_index, t2i_index):
    block = IMG_DEV * N_IMG
    grouped = feats.reshape(N_TXT, block, PATCHES, FEAT)

    def encode_block(piece):
        return encode(piece, query_states, w_query, w_key, w_value, w_out, ln_gain, w_proj)
    emb, unit, inverse = lax.map(encode_block, grouped)
    emb = emb.reshape(PAIRS, QUERIES, EMBED)
    unit = unit.reshape(PAIRS, QUERIES, EMBED)
    inverse = inverse.reshape(PAIRS, QUERIES, 1)
    text32 = text_feats.astype(jnp.float32)
    text_unit = (text32 * lax.rsqrt(lax.optimization_barrier(jnp.sum(text32 * text32, axis=-1, keepdims=True)) + 1e-06)).astype(jnp.bfloat16)
    choose = jnp.arange(QUERIES, dtype=jnp.int32)
    a_one = (i2t_index[:, None] == choose[None, :]).astype(jnp.float32)
    b_one = (t2i_index[:, None] == choose[None, :]).astype(jnp.float32)
    emb_blocks = emb.reshape(N_TXT, block, QUERIES, EMBED)
    a_blocks = a_one.reshape(N_TXT, block, QUERIES)

    def logit_block(pair):
        piece, a_piece = pair
        scores = jnp.einsum('iqe,je->iqj', piece.astype(jnp.float32), text_unit.astype(jnp.float32)) * LOGIT_SCALE
        row_part = lax.optimization_barrier(jnp.sum(scores * a_piece[:, :, None], axis=1))
        col_part = lax.optimization_barrier(jnp.sum(scores * b_one.T[None], axis=1))
        return (row_part, col_part)
    row_logit, col_logit = lax.map(logit_block, (emb_blocks, a_blocks))
    row_logit = row_logit.reshape(PAIRS, PAIRS)
    col_logit = col_logit.reshape(PAIRS, PAIRS)
    row_lse = jnp.log(lax.optimization_barrier(jnp.sum(jnp.exp(row_logit), axis=1)))
    col_lse = jnp.log(lax.optimization_barrier(jnp.sum(jnp.exp(col_logit), axis=0)))
    row_loss = row_lse - jnp.diagonal(row_logit)
    col_loss = col_lse - jnp.diagonal(col_logit)
    eye = jnp.eye(PAIRS, dtype=jnp.float32)
    g_row = (jnp.exp(row_logit - row_lse[:, None]) - eye).astype(jnp.bfloat16)
    g_col = (jnp.exp(col_logit - col_lse[None, :]) - eye).astype(jnp.bfloat16)
    text_f = text_unit.astype(jnp.float32)

    def grad_block(pair):
        row_piece, col_piece, a_piece = pair
        row_term = jnp.dot(row_piece, text_unit, preferred_element_type=jnp.float32)
        masked = col_piece.astype(jnp.float32)[None] * b_one.T[:, None, :]
        col_term = jnp.einsum('qij,jd->iqd', masked, text_f)
        return LOGIT_SCALE * (a_piece[:, :, None] * row_term[:, None, :] + col_term)
    g_emb = lax.map(grad_block, (g_row.reshape(N_TXT, block, PAIRS), g_col.reshape(N_TXT, block, PAIRS), a_blocks))
    g_emb = g_emb.reshape(PAIRS, QUERIES, EMBED)
    g_proj = (inverse * (g_emb - unit * lax.optimization_barrier(jnp.sum(unit * g_emb, axis=-1, keepdims=True)))).astype(jnp.bfloat16)
    query_grad = jnp.dot(g_proj.reshape(PAIRS * QUERIES, EMBED), w_proj.T, preferred_element_type=jnp.float32)
    query_grad = query_grad.astype(jnp.bfloat16).reshape(PAIRS, QUERIES, HIDDEN_SIZE)
    return (query_grad, row_loss, col_loss)
```

```python
import functools

import jax
import jax.numpy as jnp
from jax import lax
from jax.experimental import pallas as pl
from jax.experimental.pallas import tpu as pltpu
from jax.sharding import Mesh
from jax.sharding import PartitionSpec as P

HEAD = 64
LOGIT_SCALE = 1.0 / 0.07
GROUP = 4
PAD = 272

BF16 = jnp.bfloat16
F32 = jnp.float32


def dot(a, b):
    return jnp.dot(a, b, preferred_element_type=F32)


def dot_nt(a, b):
    return lax.dot_general(a, b, (((1,), (1,)), ((), ())), preferred_element_type=F32)


def dot_tn(a, b):
    return lax.dot_general(a, b, (((0,), (0,)), ((), ())), preferred_element_type=F32)


def encode_kernel(
    count,
    patches,
    feats_hbm,
    qs_ref,
    wq_hbm,
    wk_hbm,
    wv_hbm,
    wo_hbm,
    gain_ref,
    wp_hbm,
    unit_ref,
    inverse_ref,
    feats_ref,
    wq_ref,
    wk_ref,
    wv_ref,
    wo_ref,
    wp_ref,
    qk_ref,
    att_ref,
    sems,
):
    pairs = (
        (wq_hbm, wq_ref),
        (wk_hbm, wk_ref),
        (feats_hbm, feats_ref),
        (wv_hbm, wv_ref),
        (wo_hbm, wo_ref),
        (wp_hbm, wp_ref),
    )
    copies = [pltpu.make_async_copy(s, d, sems.at[i]) for i, (s, d) in enumerate(pairs)]
    for c in copies:
        c.start()
    queries, hidden = qs_ref.shape
    cols = GROUP * HEAD
    rows = GROUP * queries
    groups = hidden // cols
    row_head = lax.broadcasted_iota(jnp.int32, (rows, cols), 0) // queries
    col_head = lax.broadcasted_iota(jnp.int32, (rows, cols), 1) // HEAD
    own_head = row_head == col_head

    copies[0].wait()
    qhead = dot(qs_ref[...], wq_ref[...]).astype(BF16)
    copies[1].wait()
    for g in range(groups):
        piece = qhead[:, g * cols : (g + 1) * cols].astype(F32) * (HEAD**-0.5)
        tiled = jnp.concatenate([piece] * GROUP, axis=0)
        block = jnp.where(own_head, tiled, 0.0).astype(BF16)
        qk_ref[g * rows : (g + 1) * rows, :] = dot_nt(block, wk_ref[:, g * cols : (g + 1) * cols]).astype(BF16)

    copies[2].wait()
    live = lax.broadcasted_iota(jnp.int32, (PAD, groups * rows), 0) < patches
    probs = []
    for b in range(count):
        scores = dot_nt(feats_ref[b * PAD : (b + 1) * PAD, :], qk_ref[...])
        scores = jnp.where(live, scores, -jnp.inf)
        expo = jnp.exp(scores - jnp.max(scores, axis=0, keepdims=True))
        probs.append((expo / jnp.sum(expo, axis=0, keepdims=True)).astype(BF16))
    copies[3].wait()
    for b in range(count):
        values = dot(feats_ref[b * PAD : (b + 1) * PAD, :], wv_ref[...]).astype(BF16)
        for g in range(groups):
            out = dot_tn(probs[b][:, g * rows : (g + 1) * rows], values[:, g * cols : (g + 1) * cols])
            out = jnp.where(own_head, out, 0.0)
            att = sum(out[h * queries : (h + 1) * queries] for h in range(GROUP))
            att_ref[b * queries : (b + 1) * queries, g * cols : (g + 1) * cols] = att.astype(BF16)

    copies[4].wait()
    states = qs_ref[...].astype(F32)
    mixed = dot(att_ref[...], wo_ref[...]) + jnp.concatenate([states] * count, axis=0)
    centered = mixed - jnp.mean(mixed, axis=-1, keepdims=True)
    variance = jnp.mean(centered * centered, axis=-1, keepdims=True)
    q_out = centered * lax.rsqrt(variance + 1e-06) * gain_ref[...]
    copies[5].wait()
    proj = dot(q_out.astype(BF16), wp_ref[...])
    inverse = lax.rsqrt(jnp.sum(proj * proj, axis=-1, keepdims=True) + 1e-06)
    unit_ref[...] = proj * inverse
    inverse_ref[...] = inverse


def encode(feats, query_states, w_query, w_key, w_value, w_out, ln_gain, w_proj):
    count, patches, width = feats.shape
    queries, hidden = query_states.shape
    embed = w_proj.shape[1]
    padded = jnp.pad(feats, ((0, 0), (0, PAD - patches), (0, 0))).reshape(count * PAD, width)
    hbm = pl.BlockSpec(memory_space=pl.ANY)
    vmem = pl.BlockSpec(memory_space=pltpu.VMEM)
    return pl.pallas_call(
        functools.partial(encode_kernel, count, patches),
        out_shape=(
            jax.ShapeDtypeStruct((count * queries, embed), F32),
            jax.ShapeDtypeStruct((count * queries, 1), F32),
        ),
        in_specs=[hbm, vmem, hbm, hbm, hbm, hbm, vmem, hbm],
        out_specs=(vmem, vmem),
        scratch_shapes=[
            pltpu.VMEM(padded.shape, BF16),
            pltpu.VMEM(w_query.shape, BF16),
            pltpu.VMEM(w_key.shape, BF16),
            pltpu.VMEM(w_value.shape, BF16),
            pltpu.VMEM(w_out.shape, BF16),
            pltpu.VMEM(w_proj.shape, BF16),
            pltpu.VMEM((hidden // HEAD * queries, width), BF16),
            pltpu.VMEM((count * queries, hidden), BF16),
            pltpu.SemaphoreType.DMA((6,)),
        ],
        compiler_params=pltpu.CompilerParams(vmem_limit_bytes=48 * 2**20),
        cost_estimate=pl.CostEstimate(flops=int(4.0e9), bytes_accessed=int(1.1e7), transcendentals=int(5e5)),
        name="encode",
    )(padded, query_states, w_query, w_key, w_value, w_out, ln_gain.reshape(1, hidden), w_proj)


def masks(pos_ref, t2i_ref, queries, rows, texts):
    row = lax.broadcasted_iota(jnp.int32, (rows, 1), 0)
    col = lax.broadcasted_iota(jnp.int32, (1, texts), 1)
    image = row // queries
    query = row - image * queries
    chosen = query == t2i_ref[...]
    same = (image + pos_ref[0]) == col
    return image, query, chosen, same


def logits_kernel(
    count, pos_ref, i2t_ref, unit_ref, own_ref, other_ref, t2i_ref, sums_ref, row_loss_ref, text_ref, cole_ref, rowg_ref
):
    rows = unit_ref.shape[0]
    queries = rows // count
    blocks, block, _ = own_ref.shape
    texts = 2 * blocks * block
    core = pos_ref[1]
    for ref, at in ((own_ref, core), (other_ref, 1 - core)):
        for k in range(blocks):
            raw = ref[k].astype(F32)
            scale = lax.rsqrt(jnp.sum(raw * raw, axis=-1, keepdims=True) + 1e-06)
            start = pl.multiple_of((2 * k + at) * block, block)
            text_ref[pl.ds(start, block), :] = (raw * scale).astype(BF16)
    scores = dot_nt(unit_ref[...].astype(BF16), text_ref[...]) * LOGIT_SCALE
    image, query, chosen, same = masks(pos_ref, t2i_ref, queries, rows, texts)
    picked = functools.reduce(
        jnp.logical_or, [(image == b) & (query == i2t_ref[pos_ref[0] + b]) for b in range(count)]
    )
    expo = jnp.exp(scores)
    cole = jnp.where(chosen, expo, 0.0)
    cole_ref[...] = cole
    sums_ref[0:1, :] = jnp.sum(cole, axis=0, keepdims=True)
    sums_ref[1:2, :] = jnp.sum(jnp.where(chosen & same, scores, 0.0), axis=0, keepdims=True)
    row_total = jnp.sum(expo, axis=1, keepdims=True)
    row_diag = jnp.sum(jnp.where(same, scores, 0.0), axis=1, keepdims=True)
    row_loss = jnp.where(picked, jnp.log(row_total) - row_diag, 0.0)
    lane = lax.broadcasted_iota(jnp.int32, (rows, 128), 1)
    spread = jnp.sum(jnp.where(lane == image, row_loss, 0.0), axis=0, keepdims=True)
    row_loss_ref[...] = spread[:, :count]
    g_row = expo * (1.0 / row_total) - same.astype(F32)
    rowg_ref[...] = dot(jnp.where(picked, g_row, 0.0).astype(BF16), text_ref[...])


def grads_kernel(
    count,
    pos_ref,
    total_ref,
    t2i_ref,
    cole_ref,
    text_ref,
    rowg_ref,
    unit_ref,
    inverse_ref,
    wp_ref,
    grad_ref,
    col_loss_ref,
):
    rows, texts = cole_ref.shape
    queries = rows // count
    _, _, chosen, same = masks(pos_ref, t2i_ref, queries, rows, texts)
    total = total_ref[0:1, :]
    col_loss = jnp.broadcast_to(jnp.log(total) - total_ref[1:2, :], (8, texts))
    block = col_loss_ref.shape[1]
    col_loss = pltpu.roll(col_loss, texts - pos_ref[2] * block, 1)
    col_loss_ref[...] = col_loss[0:1, :block]
    g_col = cole_ref[...] * (1.0 / total) - (chosen & same).astype(F32)
    g_emb = LOGIT_SCALE * (rowg_ref[...] + dot(g_col.astype(BF16), text_ref[...]))
    unit = unit_ref[...]
    g_proj = inverse_ref[...] * (g_emb - unit * jnp.sum(unit * g_emb, axis=-1, keepdims=True))
    grad_ref[...] = dot_nt(g_proj.astype(BF16), wp_ref[...]).astype(BF16)


def spread(x, axes, n):
    return lax.all_to_all(jnp.broadcast_to(x[None], (n,) + x.shape), axes, 0, 0, tiled=True)


def swap(x):
    return lax.ppermute(x, "core", [(0, 1), (1, 0)])


def local(
    sizes,
    feats,
    query_states,
    w_query,
    w_key,
    w_value,
    w_out,
    ln_gain,
    w_proj,
    text_feats,
    i2t_index,
    t2i_index,
):
    count = feats.shape[0]
    queries, hidden = query_states.shape
    embed = w_proj.shape[1]
    block = text_feats.shape[0]
    rows = count * queries
    texts = t2i_index.shape[0]
    txt = lax.axis_index(("z", "y_hi", "core"))
    first = (lax.axis_index(("y_lo", "x")) * (texts // block) + txt) * count
    pos = jnp.stack([first, lax.axis_index("core"), txt]).astype(jnp.int32)

    own = spread(text_feats, ("z", "y_hi"), sizes["z"] * sizes["y_hi"])
    unit, inverse = encode(feats, query_states, w_query, w_key, w_value, w_out, ln_gain, w_proj)
    other = swap(own)

    vmem = pl.BlockSpec(memory_space=pltpu.VMEM)
    smem = pl.BlockSpec(memory_space=pltpu.SMEM)
    t2i = t2i_index.reshape(1, texts)
    sums, row_loss, text_unit, cole, rowg = pl.pallas_call(
        functools.partial(logits_kernel, count),
        out_shape=(
            jax.ShapeDtypeStruct((2, texts), F32),
            jax.ShapeDtypeStruct((1, count), F32),
            jax.ShapeDtypeStruct((texts, embed), BF16),
            jax.ShapeDtypeStruct((rows, texts), F32),
            jax.ShapeDtypeStruct((rows, embed), F32),
        ),
        in_specs=[smem, smem, vmem, vmem, vmem, vmem],
        out_specs=(vmem,) * 5,
        compiler_params=pltpu.CompilerParams(vmem_limit_bytes=32 * 2**20),
        name="logits",
    )(pos, i2t_index, unit, own, other, t2i)

    total = sums + swap(sums)
    total = jnp.sum(spread(total, ("y_lo", "x", "y_hi"), sizes["y_lo"] * sizes["x"] * sizes["y_hi"]), axis=0)
    total = jnp.sum(spread(total, "z", sizes["z"]), axis=0)

    query_grad, col_loss = pl.pallas_call(
        functools.partial(grads_kernel, count),
        out_shape=(
            jax.ShapeDtypeStruct((rows, hidden), BF16),
            jax.ShapeDtypeStruct((1, block), F32),
        ),
        in_specs=[smem] + [vmem] * 8,
        out_specs=(vmem, vmem),
        compiler_params=pltpu.CompilerParams(vmem_limit_bytes=32 * 2**20),
        name="grads",
    )(pos, total, t2i, cole, text_unit, rowg, unit, inverse, w_proj)
    return (
        query_grad.reshape(count, queries, hidden),
        row_loss.reshape(count),
        col_loss.reshape(block),
    )


def solution(mesh):
    sizes = {"y_lo": 2, "x": mesh.shape["img"] // 2, "z": mesh.shape["txt"] // 4, "y_hi": 2, "core": 2}
    fine = Mesh(mesh.devices.reshape(tuple(sizes.values())), tuple(sizes))
    everywhere = tuple(sizes)
    text = ("z", "y_hi", "core")
    return jax.shard_map(
        functools.partial(local, sizes),
        mesh=fine,
        in_specs=(
            P(everywhere, None, None),
            P(),
            P(),
            P(),
            P(),
            P(),
            P(),
            P(),
            P(text, None),
            P(),
            P(),
        ),
        out_specs=(P(everywhere, None, None), P(everywhere), P(text)),
        check_vma=False,
    )
```

```python
import functools

import jax
import jax.numpy as jnp
from jax import lax
from jax.experimental import pallas as pl
from jax.experimental.pallas import tpu as pltpu
from jax.sharding import Mesh
from jax.sharding import PartitionSpec as P

HEAD = 64
LOGIT_SCALE = 1.0 / 0.07
GROUP = 4

BF16 = jnp.bfloat16
F32 = jnp.float32


def dot(a, b):
    return jnp.dot(a, b, preferred_element_type=F32)


def dot_nt(a, b):
    return lax.dot_general(a, b, (((1,), (1,)), ((), ())), preferred_element_type=F32)


def dot_tn(a, b):
    return lax.dot_general(a, b, (((0,), (0,)), ((), ())), preferred_element_type=F32)


def encode_kernel(
    count,
    block,
    feats_hbm,
    qs_hbm,
    wq_hbm,
    wk_hbm,
    wv_hbm,
    wo_hbm,
    gain_hbm,
    wp_hbm,
    t2i_ref,
    proj_ref,
    turned_ref,
    feats_ref,
    qs_ref,
    wq_ref,
    wk_ref,
    wv_ref,
    wo_ref,
    gain_ref,
    wp_ref,
    flat_ref,
    qk_ref,
    values_ref,
    att_ref,
    sems,
):
    queries, hidden = qs_ref.shape
    patches, _, width = feats_ref.shape
    cols = GROUP * HEAD
    rows = GROUP * queries
    groups = hidden // cols
    total = patches * count
    texts = t2i_ref.shape[1]
    for k in range(texts // block):
        at = (k % 2) * (texts // 2) + k // 2 * block
        turned_ref[:, at : at + block] = t2i_ref[:, k * block : (k + 1) * block]
    row_head = lax.broadcasted_iota(jnp.int32, (rows, cols), 0) // queries
    col_head = lax.broadcasted_iota(jnp.int32, (rows, cols), 1) // HEAD
    own_head = row_head == col_head

    cut = patches // 2
    spans = (slice(0, cut), slice(cut, patches))
    pairs = (
        (qs_hbm, qs_ref),
        (gain_hbm, gain_ref),
        (wq_hbm, wq_ref),
        (feats_hbm.at[spans[0]], feats_ref.at[spans[0]]),
        (wv_hbm, wv_ref),
        (feats_hbm.at[spans[1]], feats_ref.at[spans[1]]),
        (wk_hbm, wk_ref),
        (wo_hbm, wo_ref),
        (wp_hbm, wp_ref),
    )
    copies = [pltpu.make_async_copy(s, d, sems.at[i]) for i, (s, d) in enumerate(pairs)]
    for c in copies:
        c.start()

    def project(p):
        lo, hi = p.start * count, p.stop * count
        flat_ref[lo:hi] = feats_ref[p].reshape(hi - lo, width)
        return lo, hi

    copies[0].wait()
    copies[2].wait()
    qhead = dot(qs_ref[...], wq_ref[...]).astype(BF16)
    copies[3].wait()
    lo, hi = project(spans[0])
    copies[4].wait()
    values_ref[lo:hi] = dot(flat_ref[lo:hi], wv_ref[...]).astype(BF16)
    copies[5].wait()
    copies[6].wait()
    lo, hi = project(spans[1])
    for g in range(groups):
        piece = qhead[:, g * cols : (g + 1) * cols].astype(F32) * (HEAD**-0.5)
        tiled = jnp.concatenate([piece] * GROUP, axis=0)
        spread_out = jnp.where(own_head, tiled, 0.0).astype(BF16)
        qk_ref[:, g * rows : (g + 1) * rows] = dot_nt(wk_ref[:, g * cols : (g + 1) * cols], spread_out).astype(BF16)
    values_ref[lo:hi] = dot(flat_ref[lo:hi], wv_ref[...]).astype(BF16)

    scores = dot(flat_ref[...], qk_ref[...])
    whole = total // 8 * 8
    body = scores[:whole].reshape(whole // 8, 8, groups * rows)
    tail = scores[whole:]
    peak8 = jnp.max(body, axis=0)
    peak = functools.reduce(jnp.maximum, [peak8[i : i + count] for i in range(0, 8, count)] + [tail])
    body = jnp.exp(body - jnp.concatenate([peak] * (8 // count), axis=0)[None])
    tail = jnp.exp(tail - peak)
    sum8 = jnp.sum(body, axis=0)
    norm = 1.0 / (sum(sum8[i : i + count] for i in range(0, 8, count)) + tail)
    body = body * jnp.concatenate([norm] * (8 // count), axis=0)[None]
    probs = jnp.concatenate([body.reshape(whole, groups * rows), tail * norm], axis=0)
    owner = lax.broadcasted_iota(jnp.int32, (rows, total), 1) % count
    for g in range(groups):
        turned = probs[:, g * rows : (g + 1) * rows].T
        parts = [jnp.where(owner == b, turned, 0.0).astype(BF16) for b in range(count)]
        out = dot(jnp.concatenate(parts, axis=0), values_ref[:, g * cols : (g + 1) * cols])
        for b in range(count):
            own = jnp.where(own_head, out[b * rows : (b + 1) * rows], 0.0)
            att = sum(own[h * queries : (h + 1) * queries] for h in range(GROUP))
            att_ref[b * queries : (b + 1) * queries, g * cols : (g + 1) * cols] = att.astype(BF16)

    copies[1].wait()
    copies[7].wait()
    states = qs_ref[...].astype(F32)
    mixed = dot(att_ref[...], wo_ref[...]) + jnp.concatenate([states] * count, axis=0)
    centered = mixed - jnp.mean(mixed, axis=-1, keepdims=True)
    variance = jnp.mean(centered * centered, axis=-1, keepdims=True)
    gain = jnp.concatenate([gain_ref[k : k + 1, :] for k in range(hidden // 128)], axis=1)
    q_out = centered * lax.rsqrt(variance + 1e-06) * gain
    copies[8].wait()
    proj_ref[...] = dot(q_out.astype(BF16), wp_ref[...])


def encode(block, feats, query_states, w_query, w_key, w_value, w_out, ln_gain, w_proj, t2i_index):
    count, patches, width = feats.shape
    queries, hidden = query_states.shape
    embed = w_proj.shape[1]
    texts = t2i_index.shape[0]
    hbm = pl.BlockSpec(memory_space=pltpu.HBM)
    vmem = pl.BlockSpec(memory_space=pltpu.VMEM)
    return pl.pallas_call(
        functools.partial(encode_kernel, count, block),
        out_shape=(
            jax.ShapeDtypeStruct((count * queries, embed), F32),
            jax.ShapeDtypeStruct((1, texts), jnp.int32),
        ),
        in_specs=[hbm] * 8 + [vmem],
        out_specs=(vmem, vmem),
        scratch_shapes=[
            pltpu.VMEM((patches, count, width), BF16),
            pltpu.VMEM(query_states.shape, BF16),
            pltpu.VMEM(w_query.shape, BF16),
            pltpu.VMEM(w_key.shape, BF16),
            pltpu.VMEM(w_value.shape, BF16),
            pltpu.VMEM(w_out.shape, BF16),
            pltpu.VMEM((hidden // 128, 128), F32),
            pltpu.VMEM(w_proj.shape, BF16),
            pltpu.VMEM((patches * count, width), BF16),
            pltpu.VMEM((width, hidden // HEAD * queries), BF16),
            pltpu.VMEM((patches * count, hidden), BF16),
            pltpu.VMEM((count * queries, hidden), BF16),
            pltpu.SemaphoreType.DMA((9,)),
        ],
        compiler_params=pltpu.CompilerParams(vmem_limit_bytes=52 * 2**20),
        cost_estimate=pl.CostEstimate(flops=int(5.5e9), bytes_accessed=int(1.1e7), transcendentals=int(5e5)),
        name="encode",
    )(
        jnp.transpose(feats, (1, 0, 2)),
        query_states,
        w_query,
        w_key,
        w_value,
        w_out,
        ln_gain.reshape(hidden // 128, 128),
        w_proj,
        t2i_index.reshape(1, texts),
    )


def normed(proj):
    inverse = lax.rsqrt(jnp.sum(proj * proj, axis=-1, keepdims=True) + 1e-06)
    return proj * inverse, inverse


def normalise_kernel(raw_ref, copies_ref):
    raw = raw_ref[...].astype(F32)
    text = (raw * lax.rsqrt(jnp.sum(raw * raw, axis=-1, keepdims=True) + 1e-06)).astype(BF16)
    for k in range(copies_ref.shape[0]):
        copies_ref[k] = text


def half_range(core, half):
    return pl.ds(pl.multiple_of(core * half, half), half)


def masks(count, rows, half, pos_ref, core, t2i):
    row = lax.broadcasted_iota(jnp.int32, (rows, 1), 0)
    col = lax.broadcasted_iota(jnp.int32, (1, half), 1)
    queries = rows // count
    image = row // queries
    chosen = row - image * queries == t2i
    same = image + (pos_ref[1] - core * half) == col
    return image, chosen, same


def logits_of(proj_ref, text):
    unit = normed(proj_ref[...])[0].astype(BF16)
    return dot_nt(unit, text) * LOGIT_SCALE


def columns(count, pos_ref, core, proj_ref, text_ref, t2i_ref, expo_ref):
    rows = proj_ref.shape[0]
    half = text_ref.shape[0]
    scores = logits_of(proj_ref, text_ref[...])
    image, chosen, same = masks(count, rows, half, pos_ref, core, t2i_ref[:, half_range(core, half)])
    expo = jnp.exp(scores)
    expo_ref[...] = expo
    total = jnp.sum(jnp.where(chosen, expo, 0.0), axis=0, keepdims=True)
    diag = jnp.sum(jnp.where(chosen & same, scores, 0.0), axis=1, keepdims=True)
    lane = lax.broadcasted_iota(jnp.int32, (rows, 128), 1)
    diag = jnp.sum(jnp.where(lane == pos_ref[4] + image, diag, 0.0), axis=0, keepdims=True)
    return total, diag


def near_kernel(count, pos_ref, proj_ref, text_ref, t2i_ref, expo_ref, sums_ref):
    half = text_ref.shape[0]
    total, diag = columns(count, pos_ref, pos_ref[2], proj_ref, text_ref, t2i_ref, expo_ref)
    sums_ref[:, :half] = total
    sums_ref[:, half:] = diag


def far_kernel(count, pos_ref, proj_ref, text_ref, t2i_ref, near_ref, expo_ref, sums_ref):
    half = text_ref.shape[0]
    core = pos_ref[2]
    total, diag = columns(count, pos_ref, 1 - core, proj_ref, text_ref, t2i_ref, expo_ref)
    sums_ref[:, half_range(core, half)] = near_ref[:, :half]
    sums_ref[:, half_range(1 - core, half)] = total
    sums_ref[:, 2 * half :] = near_ref[:, half:] + diag


def rows_kernel(
    count, pos_ref, i2t_ref, near_expo_ref, far_expo_ref, near_ref, far_ref, sums_ref, row_loss_ref, rowg_ref, again_ref
):
    again_ref[...] = sums_ref[...]
    rows, half = near_expo_ref.shape
    queries = rows // count
    core = pos_ref[2]
    row = lax.broadcasted_iota(jnp.int32, (rows, 1), 0)
    picked = functools.reduce(
        jnp.logical_or, [row == b * queries + i2t_ref[pos_ref[0] + b] for b in range(count)]
    )
    sides = ((near_ref, near_expo_ref, core), (far_ref, far_expo_ref, 1 - core))
    row_total = sum(jnp.sum(expo[...], axis=1, keepdims=True) for _, expo, _ in sides)
    scale = 1.0 / row_total
    own = 0.0
    rowg = 0.0
    for text, expo, side in sides:
        image, _, same = masks(count, rows, half, pos_ref, side, 0)
        own = own + jnp.sum(jnp.where(same, expo[...], 0.0), axis=1, keepdims=True)
        g_row = jnp.where(picked, expo[...] * scale - same.astype(F32), 0.0)
        rowg = rowg + dot(g_row.astype(BF16), text[...])
    rowg_ref[...] = rowg
    row_loss = jnp.where(picked, jnp.log(row_total) - jnp.log(own), 0.0)
    lane = lax.broadcasted_iota(jnp.int32, (rows, 128), 1)
    row_loss = jnp.sum(jnp.where(lane == image, row_loss, 0.0), axis=0, keepdims=True)
    row_loss_ref[...] = row_loss[:, :count]


def grads_kernel(
    count,
    pos_ref,
    sums_ref,
    t2i_ref,
    near_expo_ref,
    far_expo_ref,
    near_ref,
    far_ref,
    rowg_ref,
    proj_ref,
    wp_ref,
    grad_ref,
    col_loss_ref,
    total_ref,
):
    rows, half = near_expo_ref.shape
    core = pos_ref[2]
    planes = sums_ref.shape[0]
    total = sum(sums_ref[k, :, : 2 * half] for k in range(planes))
    total_ref[...] = total
    block = col_loss_ref.shape[1]
    part = block // 2
    at = pos_ref[3] * block // part
    plane, slot = at % planes, at // planes * part
    first = jnp.broadcast_to(sums_ref[plane, :, 2 * half :], (8, 128))
    second = jnp.broadcast_to(sums_ref[plane + 1, :, 2 * half :], (8, 128))
    first = pltpu.roll(first, (128 - slot) % 128, 1)
    second = pltpu.roll(second, (128 - slot + part) % 128, 1)
    lane = lax.broadcasted_iota(jnp.int32, (8, 128), 1)
    diag = jnp.where(lane < part, first, second)
    start = core * half + pos_ref[3] // 2 * block
    lse = pltpu.roll(jnp.broadcast_to(jnp.log(total), (8, 2 * half)), (2 * half - start) % (2 * half), 1)
    col_loss_ref[...] = lse[0:1, :block] - diag[0:1, :block]

    grad = rowg_ref[...]
    for text, expo, side in ((near_ref, near_expo_ref, core), (far_ref, far_expo_ref, 1 - core)):
        span = half_range(side, half)
        _, chosen, same = masks(count, rows, half, pos_ref, side, t2i_ref[:, span])
        g_col = jnp.where(chosen, expo[...] * (1.0 / total_ref[:, span]) - same.astype(F32), 0.0)
        grad = grad + dot(g_col.astype(BF16), text[...])
    g_emb = LOGIT_SCALE * grad
    unit, inverse = normed(proj_ref[...])
    g_proj = inverse * (g_emb - unit * jnp.sum(unit * g_emb, axis=-1, keepdims=True))
    grad_ref[...] = dot_nt(g_proj.astype(BF16), wp_ref[...]).astype(BF16)


def spread(x, axes, n):
    return lax.all_to_all(jnp.broadcast_to(x[None], (n,) + x.shape), axes, 0, 0, tiled=True)


def swap(x):
    return lax.ppermute(x, "core", [(0, 1), (1, 0)])


def local(
    sizes,
    feats,
    query_states,
    w_query,
    w_key,
    w_value,
    w_out,
    ln_gain,
    w_proj,
    text_feats,
    i2t_index,
    t2i_index,
):
    count = feats.shape[0]
    queries, hidden = query_states.shape
    embed = w_proj.shape[1]
    block = text_feats.shape[0]
    rows = count * queries
    texts = t2i_index.shape[0]
    half = texts // 2
    txt = lax.axis_index(("z", "y_hi", "core"))
    img = lax.axis_index(("y_lo", "x"))
    core = lax.axis_index("core")
    first = (img * (texts // block) + txt) * count
    home = first // block
    place = home % 2 * half + home // 2 * block + first % block
    slot = img * (sizes["y_hi"] * sizes["core"]) + lax.axis_index("y_hi") * sizes["core"] + core
    pos = jnp.stack([first, place, core, txt, slot * count]).astype(jnp.int32)

    vmem = pl.BlockSpec(memory_space=pltpu.VMEM)
    smem = pl.BlockSpec(memory_space=pltpu.SMEM)
    near_count = sizes["z"] * sizes["y_hi"]
    copies = pl.pallas_call(
        normalise_kernel,
        out_shape=jax.ShapeDtypeStruct((near_count,) + text_feats.shape, BF16),
        in_specs=[vmem],
        out_specs=vmem,
        compiler_params=pltpu.CompilerParams(vmem_limit_bytes=2 * 2**20),
        cost_estimate=pl.CostEstimate(flops=int(2e10), bytes_accessed=int(6e7), transcendentals=0),
        name="normalise",
    )(text_feats)
    near = lax.all_to_all(copies, ("z", "y_hi"), 0, 0, tiled=True).reshape(half, embed)
    proj, t2i = encode(
        block, feats, query_states, w_query, w_key, w_value, w_out, ln_gain, w_proj, t2i_index
    )
    far = swap(near)

    def call(kernel, name, outs, specs, flops, scratch=()):
        return pl.pallas_call(
            functools.partial(kernel, count),
            out_shape=tuple(jax.ShapeDtypeStruct(*o) for o in outs),
            in_specs=specs,
            out_specs=(vmem,) * len(outs),
            scratch_shapes=scratch,
            compiler_params=pltpu.CompilerParams(vmem_limit_bytes=16 * 2**20),
            cost_estimate=pl.CostEstimate(flops=flops, bytes_accessed=int(2e6), transcendentals=rows * texts),
            name=name,
        )

    near_expo, near_sums = call(
        near_kernel, "near", [((rows, half), F32), ((1, half + 128), F32)], [smem] + [vmem] * 3, int(2e10)
    )(pos, proj, near, t2i)
    far_expo, sums = call(
        far_kernel, "far", [((rows, half), F32), ((1, texts + 128), F32)], [smem] + [vmem] * 4, int(1e8)
    )(pos, proj, far, t2i, near_sums)
    swapped = swap(sums)
    row_loss, rowg, sums = call(
        rows_kernel,
        "rows",
        [((1, count), F32), ((rows, embed), F32), ((1, texts + 128), F32)],
        [smem] * 2 + [vmem] * 5,
        int(2e10),
    )(pos, i2t_index, near_expo, far_expo, near, far, sums)

    total = sums + swapped
    total = jnp.sum(spread(total, ("y_lo", "x", "y_hi"), sizes["y_lo"] * sizes["x"] * sizes["y_hi"]), axis=0)
    total = spread(total, "z", sizes["z"])

    query_grad, col_loss = call(
        grads_kernel,
        "grads",
        [((rows, hidden), BF16), ((1, block), F32)],
        [smem] + [vmem] * 9,
        int(2e8),
        [pltpu.VMEM((1, texts), F32)],
    )(pos, total, t2i, near_expo, far_expo, near, far, rowg, proj, w_proj)
    return (
        query_grad.reshape(count, queries, hidden),
        row_loss.reshape(count),
        col_loss.reshape(block),
    )


def solution(mesh):
    sizes = {"y_lo": 2, "x": mesh.shape["img"] // 2, "z": mesh.shape["txt"] // 4, "y_hi": 2, "core": 2}
    fine = Mesh(mesh.devices.reshape(tuple(sizes.values())), tuple(sizes))
    everywhere = tuple(sizes)
    text = ("z", "y_hi", "core")
    return jax.shard_map(
        functools.partial(local, sizes),
        mesh=fine,
        in_specs=(
            P(everywhere, None, None),
            P(),
            P(),
            P(),
            P(),
            P(),
            P(),
            P(),
            P(text, None),
            P(),
            P(),
        ),
        out_specs=(P(everywhere, None, None), P(everywhere), P(text)),
        check_vma=False,
    )
```

```python
import functools

import jax
import jax.numpy as jnp
from jax import lax
from jax.experimental import pallas as pl
from jax.experimental.pallas import tpu as pltpu
from jax.sharding import Mesh
from jax.sharding import PartitionSpec as P

HEAD = 64
LOGIT_SCALE = 1.0 / 0.07
GROUP = 4

BF16 = jnp.bfloat16
F32 = jnp.float32


def dot(a, b):
    return jnp.dot(a, b, preferred_element_type=F32)


def dot_nt(a, b):
    return lax.dot_general(a, b, (((1,), (1,)), ((), ())), preferred_element_type=F32)


def dot_tn(a, b):
    return lax.dot_general(a, b, (((0,), (0,)), ((), ())), preferred_element_type=F32)


def encode_kernel(
    count,
    block,
    feats_hbm,
    qs_hbm,
    wq_hbm,
    wk_hbm,
    wv_hbm,
    wo_hbm,
    t2i_ref,
    att_ref,
    turned_ref,
    wo_ref,
    feats_ref,
    qs_ref,
    wq_ref,
    wk_ref,
    wv_ref,
    flat_ref,
    qk_ref,
    values_ref,
    sems,
):
    queries, hidden = qs_ref.shape
    patches, _, width = feats_ref.shape
    cols = GROUP * HEAD
    rows = GROUP * queries
    groups = hidden // cols
    total = patches * count
    texts = t2i_ref.shape[1]
    for k in range(texts // block):
        at = (k % 2) * (texts // 2) + k // 2 * block
        turned_ref[:, at : at + block] = t2i_ref[:, k * block : (k + 1) * block]
    row_head = lax.broadcasted_iota(jnp.int32, (rows, cols), 0) // queries
    col_head = lax.broadcasted_iota(jnp.int32, (rows, cols), 1) // HEAD
    own_head = row_head == col_head

    cut = patches // 2
    spans = (slice(0, cut), slice(cut, patches))
    pairs = (
        (qs_hbm, qs_ref),
        (wq_hbm, wq_ref),
        (wk_hbm, wk_ref),
        (feats_hbm.at[spans[0]], feats_ref.at[spans[0]]),
        (feats_hbm.at[spans[1]], feats_ref.at[spans[1]]),
        (wv_hbm, wv_ref),
        (wo_hbm, wo_ref),
    )
    copies = [pltpu.make_async_copy(s, d, sems.at[i]) for i, (s, d) in enumerate(pairs)]
    for c in copies:
        c.start()

    def project(p):
        lo, hi = p.start * count, p.stop * count
        flat_ref[lo:hi] = feats_ref[p].reshape(hi - lo, width)
        return lo, hi

    copies[0].wait()
    copies[1].wait()
    qhead = dot(qs_ref[...], wq_ref[...]).astype(BF16)
    copies[2].wait()
    for g in range(groups):
        piece = qhead[:, g * cols : (g + 1) * cols].astype(F32) * (HEAD**-0.5)
        tiled = jnp.concatenate([piece] * GROUP, axis=0)
        spread_out = jnp.where(own_head, tiled, 0.0).astype(BF16)
        qk_ref[:, g * rows : (g + 1) * rows] = dot_nt(wk_ref[:, g * cols : (g + 1) * cols], spread_out).astype(BF16)
    copies[3].wait()
    project(spans[0])
    copies[4].wait()
    project(spans[1])
    scores = dot(flat_ref[...], qk_ref[...])
    copies[5].wait()
    whole = total // 8 * 8
    body = scores[:whole].reshape(whole // 8, 8, groups * rows)
    tail = scores[whole:]
    peak8 = jnp.max(body, axis=0)
    peak = functools.reduce(jnp.maximum, [peak8[i : i + count] for i in range(0, 8, count)] + [tail])
    body = jnp.exp(body - jnp.concatenate([peak] * (8 // count), axis=0)[None])
    tail = jnp.exp(tail - peak)
    sum8 = jnp.sum(body, axis=0)
    norm = 1.0 / (sum(sum8[i : i + count] for i in range(0, 8, count)) + tail)
    norm = jnp.concatenate([norm] * (8 // count), axis=0)
    probs = jnp.concatenate([body.reshape(whole, groups * rows), tail], axis=0).astype(BF16)
    values_ref[...] = dot(flat_ref[...], wv_ref[...]).astype(BF16)
    owner = lax.broadcasted_iota(jnp.int32, (rows, total), 1) % count
    owns = [(owner == b).astype(F32).astype(BF16) for b in range(count)]
    for g in range(groups):
        turned = probs[:, g * rows : (g + 1) * rows].T
        parts = [turned * owns[b] for b in range(count)]
        out = dot(jnp.concatenate(parts, axis=0), values_ref[:, g * cols : (g + 1) * cols])
        scale = norm[:, g * rows : (g + 1) * rows].T
        for b in range(count):
            own = jnp.where(own_head, out[b * rows : (b + 1) * rows] * scale[:, b : b + 1], 0.0)
            att = sum(own[h * queries : (h + 1) * queries] for h in range(GROUP))
            att_ref[b * queries : (b + 1) * queries, g * cols : (g + 1) * cols] = att.astype(BF16)
    copies[6].wait()


def encode(block, feats, query_states, w_query, w_key, w_value, w_out, t2i_index):
    count, patches, width = feats.shape
    queries, hidden = query_states.shape
    texts = t2i_index.shape[0]
    hbm = pl.BlockSpec(memory_space=pltpu.HBM)
    vmem = pl.BlockSpec(memory_space=pltpu.VMEM)
    return pl.pallas_call(
        functools.partial(encode_kernel, count, block),
        out_shape=(
            jax.ShapeDtypeStruct((count * queries, hidden), BF16),
            jax.ShapeDtypeStruct((1, texts), jnp.int32),
            jax.ShapeDtypeStruct(w_out.shape, BF16),
        ),
        in_specs=[hbm] * 6 + [vmem],
        out_specs=(vmem, vmem, vmem),
        scratch_shapes=[
            pltpu.VMEM((patches, count, width), BF16),
            pltpu.VMEM(query_states.shape, BF16),
            pltpu.VMEM(w_query.shape, BF16),
            pltpu.VMEM(w_key.shape, BF16),
            pltpu.VMEM(w_value.shape, BF16),
            pltpu.VMEM((patches * count, width), BF16),
            pltpu.VMEM((width, hidden // HEAD * queries), BF16),
            pltpu.VMEM((patches * count, hidden), BF16),
            pltpu.SemaphoreType.DMA((7,)),
        ],
        compiler_params=pltpu.CompilerParams(vmem_limit_bytes=52 * 2**20),
        cost_estimate=pl.CostEstimate(flops=int(5.5e9), bytes_accessed=int(1.1e7), transcendentals=int(5e5)),
        name="encode",
    )(
        jnp.transpose(feats, (1, 0, 2)),
        query_states,
        w_query,
        w_key,
        w_value,
        w_out,
        t2i_index.reshape(1, texts),
    )


def normed(proj):
    inverse = lax.rsqrt(jnp.sum(proj * proj, axis=-1, keepdims=True) + 1e-06)
    return proj * inverse, inverse


def normalise_kernel(raw_ref, copies_ref):
    raw = raw_ref[...].astype(F32)
    text = (raw * lax.rsqrt(jnp.sum(raw * raw, axis=-1, keepdims=True) + 1e-06)).astype(BF16)
    for k in range(copies_ref.shape[0]):
        copies_ref[k] = text


def half_range(core, half):
    return pl.ds(pl.multiple_of(core * half, half), half)


def masks(count, rows, half, pos_ref, core, t2i):
    row = lax.broadcasted_iota(jnp.int32, (rows, 1), 0)
    col = lax.broadcasted_iota(jnp.int32, (1, half), 1)
    queries = rows // count
    image = row // queries
    chosen = row - image * queries == t2i
    same = image + (pos_ref[1] - core * half) == col
    return image, chosen, same


def logits_of(proj_ref, text):
    unit = normed(proj_ref[...])[0].astype(BF16)
    return dot_nt(unit, text) * LOGIT_SCALE


def columns(count, pos_ref, core, proj_ref, text_ref, t2i_ref, expo_ref):
    rows = proj_ref.shape[0]
    half = text_ref.shape[0]
    scores = logits_of(proj_ref, text_ref[...])
    image, chosen, same = masks(count, rows, half, pos_ref, core, t2i_ref[:, half_range(core, half)])
    expo = jnp.exp(scores)
    expo_ref[...] = expo
    total = jnp.sum(jnp.where(chosen, expo, 0.0), axis=0, keepdims=True)
    diag = jnp.sum(jnp.where(chosen & same, scores, 0.0), axis=1, keepdims=True)
    lane = lax.broadcasted_iota(jnp.int32, (rows, 128), 1)
    diag = jnp.sum(jnp.where(lane == pos_ref[4] + image, diag, 0.0), axis=0, keepdims=True)
    return total, diag


def near_kernel(
    count,
    pos_ref,
    att_ref,
    qs_ref,
    wo_ref,
    gain_ref,
    wp_ref,
    text_ref,
    t2i_ref,
    proj_ref,
    expo_ref,
    sums_ref,
):
    hidden = att_ref.shape[1]
    states = qs_ref[...].astype(F32)
    mixed = dot(att_ref[...], wo_ref[...]) + jnp.concatenate([states] * count, axis=0)
    centered = mixed - jnp.mean(mixed, axis=-1, keepdims=True)
    variance = jnp.mean(centered * centered, axis=-1, keepdims=True)
    gain = jnp.concatenate([gain_ref[k : k + 1, :] for k in range(hidden // 128)], axis=1)
    q_out = centered * lax.rsqrt(variance + 1e-06) * gain
    proj_ref[...] = dot(q_out.astype(BF16), wp_ref[...])
    half = text_ref.shape[0]
    total, diag = columns(count, pos_ref, pos_ref[2], proj_ref, text_ref, t2i_ref, expo_ref)
    sums_ref[:, :half] = total
    sums_ref[:, half:] = diag


def far_kernel(count, pos_ref, proj_ref, text_ref, t2i_ref, near_ref, expo_ref, sums_ref):
    half = text_ref.shape[0]
    core = pos_ref[2]
    total, diag = columns(count, pos_ref, 1 - core, proj_ref, text_ref, t2i_ref, expo_ref)
    sums_ref[:, half_range(core, half)] = near_ref[:, :half]
    sums_ref[:, half_range(1 - core, half)] = total
    sums_ref[:, 2 * half :] = near_ref[:, half:] + diag


def rows_kernel(
    count, pos_ref, i2t_ref, near_expo_ref, far_expo_ref, near_ref, far_ref, sums_ref, row_loss_ref, rowg_ref, again_ref
):
    again_ref[...] = sums_ref[...]
    rows, half = near_expo_ref.shape
    queries = rows // count
    core = pos_ref[2]
    row = lax.broadcasted_iota(jnp.int32, (rows, 1), 0)
    picked = functools.reduce(
        jnp.logical_or, [row == b * queries + i2t_ref[pos_ref[0] + b] for b in range(count)]
    )
    sides = ((near_ref, near_expo_ref, core), (far_ref, far_expo_ref, 1 - core))
    row_total = sum(jnp.sum(expo[...], axis=1, keepdims=True) for _, expo, _ in sides)
    scale = 1.0 / row_total
    own = 0.0
    rowg = 0.0
    for text, expo, side in sides:
        image, _, same = masks(count, rows, half, pos_ref, side, 0)
        own = own + jnp.sum(jnp.where(same, expo[...], 0.0), axis=1, keepdims=True)
        g_row = jnp.where(picked, expo[...] * scale - same.astype(F32), 0.0)
        rowg = rowg + dot(g_row.astype(BF16), text[...])
    rowg_ref[...] = rowg
    row_loss = jnp.where(picked, jnp.log(row_total) - jnp.log(own), 0.0)
    lane = lax.broadcasted_iota(jnp.int32, (rows, 128), 1)
    row_loss = jnp.sum(jnp.where(lane == image, row_loss, 0.0), axis=0, keepdims=True)
    row_loss_ref[...] = row_loss[:, :count]


def grads_kernel(
    count,
    pos_ref,
    sums_ref,
    t2i_ref,
    near_expo_ref,
    far_expo_ref,
    near_ref,
    far_ref,
    rowg_ref,
    proj_ref,
    wp_ref,
    grad_ref,
    col_loss_ref,
    total_ref,
):
    rows, half = near_expo_ref.shape
    core = pos_ref[2]
    planes = sums_ref.shape[0]
    total = sum(sums_ref[k, :, : 2 * half] for k in range(planes))
    total_ref[...] = total
    block = col_loss_ref.shape[1]
    part = block // 2
    at = pos_ref[3] * block // part
    plane, slot = at % planes, at // planes * part
    first = jnp.broadcast_to(sums_ref[plane, :, 2 * half :], (8, 128))
    second = jnp.broadcast_to(sums_ref[plane + 1, :, 2 * half :], (8, 128))
    first = pltpu.roll(first, (128 - slot) % 128, 1)
    second = pltpu.roll(second, (128 - slot + part) % 128, 1)
    lane = lax.broadcasted_iota(jnp.int32, (8, 128), 1)
    diag = jnp.where(lane < part, first, second)
    start = core * half + pos_ref[3] // 2 * block
    lse = pltpu.roll(jnp.broadcast_to(jnp.log(total), (8, 2 * half)), (2 * half - start) % (2 * half), 1)
    col_loss_ref[...] = lse[0:1, :block] - diag[0:1, :block]

    grad = rowg_ref[...]
    for text, expo, side in ((near_ref, near_expo_ref, core), (far_ref, far_expo_ref, 1 - core)):
        span = half_range(side, half)
        _, chosen, same = masks(count, rows, half, pos_ref, side, t2i_ref[:, span])
        g_col = jnp.where(chosen, expo[...] * (1.0 / total_ref[:, span]) - same.astype(F32), 0.0)
        grad = grad + dot(g_col.astype(BF16), text[...])
    g_emb = LOGIT_SCALE * grad
    unit, inverse = normed(proj_ref[...])
    g_proj = inverse * (g_emb - unit * jnp.sum(unit * g_emb, axis=-1, keepdims=True))
    grad_ref[...] = dot_nt(g_proj.astype(BF16), wp_ref[...]).astype(BF16)


def spread(x, axes, n):
    return lax.all_to_all(jnp.broadcast_to(x[None], (n,) + x.shape), axes, 0, 0, tiled=True)


def text_groups(sizes):
    z, hi = sizes["z"], sizes["y_hi"]
    return [[((side ^ h) * z + k) * hi + h for k in range(z) for h in range(hi)] for side in range(hi)]


def swap(x):
    return lax.ppermute(x, "core", [(0, 1), (1, 0)])


def local(
    sizes,
    feats,
    query_states,
    w_query,
    w_key,
    w_value,
    w_out,
    ln_gain,
    w_proj,
    text_feats,
    i2t_index,
    t2i_index,
):
    count = feats.shape[0]
    queries, hidden = query_states.shape
    embed = w_proj.shape[1]
    block = text_feats.shape[0]
    rows = count * queries
    texts = t2i_index.shape[0]
    half = texts // 2
    txt = lax.axis_index(("z", "y_hi", "core"))
    img = lax.axis_index(("y_lo", "x"))
    core = lax.axis_index("core")
    first = (img * (texts // block) + txt) * count
    home = first // block
    place = home % 2 * half + home // 2 * block + first % block
    slot = img * (sizes["y_hi"] * sizes["core"]) + lax.axis_index("y_hi") * sizes["core"] + core
    pos = jnp.stack([first, place, core, txt, slot * count]).astype(jnp.int32)

    vmem = pl.BlockSpec(memory_space=pltpu.VMEM)
    smem = pl.BlockSpec(memory_space=pltpu.SMEM)
    near_count = sizes["z"] * sizes["y_hi"]
    copies = pl.pallas_call(
        normalise_kernel,
        out_shape=jax.ShapeDtypeStruct((near_count,) + text_feats.shape, BF16),
        in_specs=[vmem],
        out_specs=vmem,
        compiler_params=pltpu.CompilerParams(vmem_limit_bytes=2 * 2**20),
        cost_estimate=pl.CostEstimate(flops=int(2e10), bytes_accessed=int(6e7), transcendentals=0),
        name="normalise",
    )(text_feats)
    near = lax.all_to_all(
        copies, ("y_lo", "z", "y_hi"), 0, 0, axis_index_groups=text_groups(sizes), tiled=True
    ).reshape(half, embed)
    att, t2i, w_out = encode(block, feats, query_states, w_query, w_key, w_value, w_out, t2i_index)
    far = swap(near)

    def call(kernel, name, outs, specs, flops, scratch=()):
        return pl.pallas_call(
            functools.partial(kernel, count),
            out_shape=tuple(jax.ShapeDtypeStruct(*o) for o in outs),
            in_specs=specs,
            out_specs=(vmem,) * len(outs),
            scratch_shapes=scratch,
            compiler_params=pltpu.CompilerParams(vmem_limit_bytes=16 * 2**20),
            cost_estimate=pl.CostEstimate(flops=flops, bytes_accessed=int(2e6), transcendentals=rows * texts),
            name=name,
        )

    proj, near_expo, near_sums = call(
        near_kernel,
        "near",
        [((rows, embed), F32), ((rows, half), F32), ((1, half + 128), F32)],
        [smem] + [vmem] * 7,
        int(2e10),
    )(pos, att, query_states, w_out, ln_gain.reshape(hidden // 128, 128), w_proj, near, t2i)
    far_expo, sums = call(
        far_kernel, "far", [((rows, half), F32), ((1, texts + 128), F32)], [smem] + [vmem] * 4, int(1e8)
    )(pos, proj, far, t2i, near_sums)
    swapped = swap(sums)
    row_loss, rowg, sums = call(
        rows_kernel,
        "rows",
        [((1, count), F32), ((rows, embed), F32), ((1, texts + 128), F32)],
        [smem] * 2 + [vmem] * 5,
        int(2e10),
    )(pos, i2t_index, near_expo, far_expo, near, far, sums)

    total = sums + swapped
    total = jnp.sum(spread(total, ("y_lo", "x", "y_hi"), sizes["y_lo"] * sizes["x"] * sizes["y_hi"]), axis=0)
    total = spread(total, "z", sizes["z"])

    query_grad, col_loss = call(
        grads_kernel,
        "grads",
        [((rows, hidden), BF16), ((1, block), F32)],
        [smem] + [vmem] * 9,
        int(2e8),
        [pltpu.VMEM((1, texts), F32)],
    )(pos, total, t2i, near_expo, far_expo, near, far, rowg, proj, w_proj)
    return (
        query_grad.reshape(count, queries, hidden),
        row_loss.reshape(count),
        col_loss.reshape(block),
    )


def solution(mesh):
    sizes = {"y_lo": 2, "x": mesh.shape["img"] // 2, "z": mesh.shape["txt"] // 4, "y_hi": 2, "core": 2}
    fine = Mesh(mesh.devices.reshape(tuple(sizes.values())), tuple(sizes))
    everywhere = tuple(sizes)
    text = ("z", "y_hi", "core")
    return jax.shard_map(
        functools.partial(local, sizes),
        mesh=fine,
        in_specs=(
            P(everywhere, None, None),
            P(),
            P(),
            P(),
            P(),
            P(),
            P(),
            P(),
            P(text, None),
            P(),
            P(),
        ),
        out_specs=(P(everywhere, None, None), P(everywhere), P(text)),
        check_vma=False,
    )
```

```python
import functools

import jax
import jax.numpy as jnp
from jax import lax
from jax.experimental import pallas as pl
from jax.experimental.pallas import tpu as pltpu
from jax.sharding import Mesh
from jax.sharding import PartitionSpec as P

HEAD = 64
LOGIT_SCALE = 1.0 / 0.07
GROUP = 4

BF16 = jnp.bfloat16
F32 = jnp.float32


def dot(a, b):
    return jnp.dot(a, b, preferred_element_type=F32)


def dot_nt(a, b):
    return lax.dot_general(a, b, (((1,), (1,)), ((), ())), preferred_element_type=F32)


def dot_tn(a, b):
    return lax.dot_general(a, b, (((0,), (0,)), ((), ())), preferred_element_type=F32)


def encode_kernel(
    count,
    block,
    feats_hbm,
    qs_hbm,
    wq_hbm,
    wk_hbm,
    wv_hbm,
    wo_hbm,
    t2i_ref,
    mixed_ref,
    turned_ref,
    feats_ref,
    qs_ref,
    wq_ref,
    wk_ref,
    wv_ref,
    flat_ref,
    qk_ref,
    values_ref,
    wo_ref,
    att_ref,
    sems,
):
    queries, hidden = qs_ref.shape
    patches, _, width = feats_ref.shape
    cols = GROUP * HEAD
    rows = GROUP * queries
    groups = hidden // cols
    total = patches * count
    texts = t2i_ref.shape[1]
    for k in range(texts // block):
        at = (k % 2) * (texts // 2) + k // 2 * block
        turned_ref[:, at : at + block] = t2i_ref[:, k * block : (k + 1) * block]
    row_head = lax.broadcasted_iota(jnp.int32, (rows, cols), 0) // queries
    col_head = lax.broadcasted_iota(jnp.int32, (rows, cols), 1) // HEAD
    own_head = row_head == col_head

    cut = patches // 2
    spans = (slice(0, cut), slice(cut, patches))
    pairs = (
        (qs_hbm, qs_ref),
        (wq_hbm, wq_ref),
        (wk_hbm, wk_ref),
        (feats_hbm.at[spans[0]], feats_ref.at[spans[0]]),
        (feats_hbm.at[spans[1]], feats_ref.at[spans[1]]),
        (wv_hbm, wv_ref),
        (wo_hbm, wo_ref),
    )
    copies = [pltpu.make_async_copy(s, d, sems.at[i]) for i, (s, d) in enumerate(pairs)]
    for c in copies:
        c.start()

    def project(p):
        lo, hi = p.start * count, p.stop * count
        flat_ref[lo:hi] = feats_ref[p].reshape(hi - lo, width)
        return lo, hi

    copies[0].wait()
    copies[1].wait()
    qhead = dot(qs_ref[...], wq_ref[...]).astype(BF16)
    copies[2].wait()
    for g in range(groups):
        piece = qhead[:, g * cols : (g + 1) * cols].astype(F32) * (HEAD**-0.5)
        tiled = jnp.concatenate([piece] * GROUP, axis=0)
        spread_out = jnp.where(own_head, tiled, 0.0).astype(BF16)
        qk_ref[:, g * rows : (g + 1) * rows] = dot_nt(wk_ref[:, g * cols : (g + 1) * cols], spread_out).astype(BF16)
    copies[3].wait()
    copies[4].wait()
    project(spans[0])
    project(spans[1])
    scores = dot(flat_ref[...], qk_ref[...])
    copies[5].wait()
    copies[6].wait()
    whole = total // 8 * 8
    body = scores[:whole].reshape(whole // 8, 8, groups * rows)
    tail = scores[whole:]
    peak8 = jnp.max(body, axis=0)
    peak = functools.reduce(jnp.maximum, [peak8[i : i + count] for i in range(0, 8, count)] + [tail])
    body = jnp.exp(body - jnp.concatenate([peak] * (8 // count), axis=0)[None])
    tail = jnp.exp(tail - peak)
    sum8 = jnp.sum(body, axis=0)
    norm = 1.0 / (sum(sum8[i : i + count] for i in range(0, 8, count)) + tail)
    norm = jnp.concatenate([norm] * (8 // count), axis=0)
    probs = jnp.concatenate([body.reshape(whole, groups * rows), tail], axis=0).astype(BF16)
    values_ref[...] = dot(flat_ref[...], wv_ref[...]).astype(BF16)
    owner = lax.broadcasted_iota(jnp.int32, (rows, total), 1) % count
    owns = [(owner == b).astype(F32).astype(BF16) for b in range(count)]
    for g in range(groups):
        turned = probs[:, g * rows : (g + 1) * rows].T
        parts = [turned * owns[b] for b in range(count)]
        out = dot(jnp.concatenate(parts, axis=0), values_ref[:, g * cols : (g + 1) * cols])
        scale = norm[:, g * rows : (g + 1) * rows].T
        for b in range(count):
            own = jnp.where(own_head, out[b * rows : (b + 1) * rows] * scale[:, b : b + 1], 0.0)
            att = sum(own[h * queries : (h + 1) * queries] for h in range(GROUP))
            att_ref[b * queries : (b + 1) * queries, g * cols : (g + 1) * cols] = att.astype(BF16)
    states = qs_ref[...].astype(F32)
    mixed_ref[...] = dot(att_ref[...], wo_ref[...]) + jnp.concatenate([states] * count, axis=0)


def encode(block, feats, query_states, w_query, w_key, w_value, w_out, t2i_index):
    count, patches, width = feats.shape
    queries, hidden = query_states.shape
    texts = t2i_index.shape[0]
    hbm = pl.BlockSpec(memory_space=pltpu.HBM)
    vmem = pl.BlockSpec(memory_space=pltpu.VMEM)
    return pl.pallas_call(
        functools.partial(encode_kernel, count, block),
        out_shape=(
            jax.ShapeDtypeStruct((count * queries, hidden), F32),
            jax.ShapeDtypeStruct((1, texts), jnp.int32),
        ),
        in_specs=[hbm] * 6 + [vmem],
        out_specs=(vmem, vmem),
        scratch_shapes=[
            pltpu.VMEM((patches, count, width), BF16),
            pltpu.VMEM(query_states.shape, BF16),
            pltpu.VMEM(w_query.shape, BF16),
            pltpu.VMEM(w_key.shape, BF16),
            pltpu.VMEM(w_value.shape, BF16),
            pltpu.VMEM((patches * count, width), BF16),
            pltpu.VMEM((width, hidden // HEAD * queries), BF16),
            pltpu.VMEM((patches * count, hidden), BF16),
            pltpu.VMEM(w_out.shape, BF16),
            pltpu.VMEM((count * queries, hidden), BF16),
            pltpu.SemaphoreType.DMA((7,)),
        ],
        compiler_params=pltpu.CompilerParams(vmem_limit_bytes=52 * 2**20),
        cost_estimate=pl.CostEstimate(flops=int(5.5e9), bytes_accessed=int(1.1e7), transcendentals=int(5e5)),
        name="encode",
    )(
        jnp.transpose(feats, (1, 0, 2)),
        query_states,
        w_query,
        w_key,
        w_value,
        w_out,
        t2i_index.reshape(1, texts),
    )


def normed(proj):
    inverse = lax.rsqrt(jnp.sum(proj * proj, axis=-1, keepdims=True) + 1e-06)
    return proj * inverse, inverse


def normalise_kernel(raw_ref, copies_ref):
    raw = raw_ref[...].astype(F32)
    text = (raw * lax.rsqrt(jnp.sum(raw * raw, axis=-1, keepdims=True) + 1e-06)).astype(BF16)
    for k in range(copies_ref.shape[0]):
        copies_ref[k] = text


def half_range(core, half):
    return pl.ds(pl.multiple_of(core * half, half), half)


def masks(count, rows, half, pos_ref, core, t2i):
    row = lax.broadcasted_iota(jnp.int32, (rows, 1), 0)
    col = lax.broadcasted_iota(jnp.int32, (1, half), 1)
    queries = rows // count
    image = row // queries
    chosen = row - image * queries == t2i
    same = image + (pos_ref[1] - core * half) == col
    return image, chosen, same


def logits_of(proj_ref, text):
    unit = normed(proj_ref[...])[0].astype(BF16)
    return dot_nt(unit, text) * LOGIT_SCALE


def columns(count, pos_ref, core, proj_ref, text_ref, t2i_ref, expo_ref):
    rows = proj_ref.shape[0]
    half = text_ref.shape[0]
    scores = logits_of(proj_ref, text_ref[...])
    image, chosen, same = masks(count, rows, half, pos_ref, core, t2i_ref[:, half_range(core, half)])
    expo = jnp.exp(scores)
    expo_ref[...] = expo
    total = jnp.sum(jnp.where(chosen, expo, 0.0), axis=0, keepdims=True)
    diag = jnp.sum(jnp.where(chosen & same, scores, 0.0), axis=1, keepdims=True)
    lane = lax.broadcasted_iota(jnp.int32, (rows, 128), 1)
    diag = jnp.sum(jnp.where(lane == pos_ref[4] + image, diag, 0.0), axis=0, keepdims=True)
    return total, diag


def near_kernel(
    count,
    pos_ref,
    mixed_ref,
    gain_ref,
    wp_ref,
    text_ref,
    t2i_ref,
    proj_ref,
    expo_ref,
    sums_ref,
):
    hidden = mixed_ref.shape[1]
    mixed = mixed_ref[...]
    centered = mixed - jnp.mean(mixed, axis=-1, keepdims=True)
    variance = jnp.mean(centered * centered, axis=-1, keepdims=True)
    gain = jnp.concatenate([gain_ref[k : k + 1, :] for k in range(hidden // 128)], axis=1)
    q_out = centered * lax.rsqrt(variance + 1e-06) * gain
    proj_ref[...] = dot(q_out.astype(BF16), wp_ref[...])
    half = text_ref.shape[0]
    total, diag = columns(count, pos_ref, pos_ref[2], proj_ref, text_ref, t2i_ref, expo_ref)
    sums_ref[:, :half] = total
    sums_ref[:, half:] = diag


def far_kernel(count, pos_ref, proj_ref, text_ref, t2i_ref, near_ref, expo_ref, sums_ref):
    half = text_ref.shape[0]
    core = pos_ref[2]
    total, diag = columns(count, pos_ref, 1 - core, proj_ref, text_ref, t2i_ref, expo_ref)
    sums_ref[:, half_range(core, half)] = near_ref[:, :half]
    sums_ref[:, half_range(1 - core, half)] = total
    sums_ref[:, 2 * half :] = near_ref[:, half:] + diag


def rows_kernel(
    count, pos_ref, i2t_ref, near_expo_ref, far_expo_ref, near_ref, far_ref, sums_ref, row_loss_ref, rowg_ref, again_ref
):
    again_ref[...] = sums_ref[...]
    rows, half = near_expo_ref.shape
    queries = rows // count
    core = pos_ref[2]
    row = lax.broadcasted_iota(jnp.int32, (rows, 1), 0)
    picked = functools.reduce(
        jnp.logical_or, [row == b * queries + i2t_ref[pos_ref[0] + b] for b in range(count)]
    )
    sides = ((near_ref, near_expo_ref, core), (far_ref, far_expo_ref, 1 - core))
    row_total = sum(jnp.sum(expo[...], axis=1, keepdims=True) for _, expo, _ in sides)
    scale = 1.0 / row_total
    own = 0.0
    rowg = 0.0
    for text, expo, side in sides:
        image, _, same = masks(count, rows, half, pos_ref, side, 0)
        own = own + jnp.sum(jnp.where(same, expo[...], 0.0), axis=1, keepdims=True)
        g_row = jnp.where(picked, expo[...] * scale - same.astype(F32), 0.0)
        rowg = rowg + dot(g_row.astype(BF16), text[...])
    rowg_ref[...] = rowg
    row_loss = jnp.where(picked, jnp.log(row_total) - jnp.log(own), 0.0)
    lane = lax.broadcasted_iota(jnp.int32, (rows, 128), 1)
    row_loss = jnp.sum(jnp.where(lane == image, row_loss, 0.0), axis=0, keepdims=True)
    row_loss_ref[...] = row_loss[:, :count]


def grads_kernel(
    count,
    pos_ref,
    sums_ref,
    t2i_ref,
    near_expo_ref,
    far_expo_ref,
    near_ref,
    far_ref,
    rowg_ref,
    proj_ref,
    wp_ref,
    grad_ref,
    col_loss_ref,
    total_ref,
):
    rows, half = near_expo_ref.shape
    core = pos_ref[2]
    planes = sums_ref.shape[0]
    total = sum(sums_ref[k, :, : 2 * half] for k in range(planes))
    total_ref[...] = total
    block = col_loss_ref.shape[1]
    part = block // 2
    at = pos_ref[3] * block // part
    plane, slot = at % planes, at // planes * part
    first = jnp.broadcast_to(sums_ref[plane, :, 2 * half :], (8, 128))
    second = jnp.broadcast_to(sums_ref[plane + 1, :, 2 * half :], (8, 128))
    first = pltpu.roll(first, (128 - slot) % 128, 1)
    second = pltpu.roll(second, (128 - slot + part) % 128, 1)
    lane = lax.broadcasted_iota(jnp.int32, (8, 128), 1)
    diag = jnp.where(lane < part, first, second)
    start = core * half + pos_ref[3] // 2 * block
    lse = pltpu.roll(jnp.broadcast_to(jnp.log(total), (8, 2 * half)), (2 * half - start) % (2 * half), 1)
    col_loss_ref[...] = lse[0:1, :block] - diag[0:1, :block]

    grad = rowg_ref[...]
    for text, expo, side in ((near_ref, near_expo_ref, core), (far_ref, far_expo_ref, 1 - core)):
        span = half_range(side, half)
        _, chosen, same = masks(count, rows, half, pos_ref, side, t2i_ref[:, span])
        g_col = jnp.where(chosen, expo[...] * (1.0 / total_ref[:, span]) - same.astype(F32), 0.0)
        grad = grad + dot(g_col.astype(BF16), text[...])
    g_emb = LOGIT_SCALE * grad
    unit, inverse = normed(proj_ref[...])
    g_proj = inverse * (g_emb - unit * jnp.sum(unit * g_emb, axis=-1, keepdims=True))
    grad_ref[...] = dot_nt(g_proj.astype(BF16), wp_ref[...]).astype(BF16)


def spread(x, axes, n):
    return lax.all_to_all(jnp.broadcast_to(x[None], (n,) + x.shape), axes, 0, 0, tiled=True)


def text_groups(sizes):
    z, hi = sizes["z"], sizes["y_hi"]
    return [[((side ^ h) * z + k) * hi + h for k in range(z) for h in range(hi)] for side in range(hi)]


def swap(x):
    return lax.ppermute(x, "core", [(0, 1), (1, 0)])


def local(
    sizes,
    feats,
    query_states,
    w_query,
    w_key,
    w_value,
    w_out,
    ln_gain,
    w_proj,
    text_feats,
    i2t_index,
    t2i_index,
):
    count = feats.shape[0]
    queries, hidden = query_states.shape
    embed = w_proj.shape[1]
    block = text_feats.shape[0]
    rows = count * queries
    texts = t2i_index.shape[0]
    half = texts // 2
    txt = lax.axis_index(("z", "y_hi", "core"))
    img = lax.axis_index(("y_lo", "x"))
    core = lax.axis_index("core")
    first = (img * (texts // block) + txt) * count
    home = first // block
    place = home % 2 * half + home // 2 * block + first % block
    slot = img * (sizes["y_hi"] * sizes["core"]) + lax.axis_index("y_hi") * sizes["core"] + core
    pos = jnp.stack([first, place, core, txt, slot * count]).astype(jnp.int32)

    vmem = pl.BlockSpec(memory_space=pltpu.VMEM)
    smem = pl.BlockSpec(memory_space=pltpu.SMEM)
    near_count = sizes["z"] * sizes["y_hi"]
    copies = pl.pallas_call(
        normalise_kernel,
        out_shape=jax.ShapeDtypeStruct((near_count,) + text_feats.shape, BF16),
        in_specs=[vmem],
        out_specs=vmem,
        compiler_params=pltpu.CompilerParams(vmem_limit_bytes=2 * 2**20),
        cost_estimate=pl.CostEstimate(flops=int(2e10), bytes_accessed=int(6e7), transcendentals=0),
        name="normalise",
    )(text_feats)
    near = lax.all_to_all(
        copies, ("y_lo", "z", "y_hi"), 0, 0, axis_index_groups=text_groups(sizes), tiled=True
    ).reshape(half, embed)
    mixed, t2i = encode(block, feats, query_states, w_query, w_key, w_value, w_out, t2i_index)
    far = swap(near)

    def call(kernel, name, outs, specs, flops, scratch=()):
        return pl.pallas_call(
            functools.partial(kernel, count),
            out_shape=tuple(jax.ShapeDtypeStruct(*o) for o in outs),
            in_specs=specs,
            out_specs=(vmem,) * len(outs),
            scratch_shapes=scratch,
            compiler_params=pltpu.CompilerParams(vmem_limit_bytes=16 * 2**20),
            cost_estimate=pl.CostEstimate(flops=flops, bytes_accessed=int(2e6), transcendentals=rows * texts),
            name=name,
        )

    proj, near_expo, near_sums = call(
        near_kernel,
        "near",
        [((rows, embed), F32), ((rows, half), F32), ((1, half + 128), F32)],
        [smem] + [vmem] * 5,
        int(2e10),
    )(pos, mixed, ln_gain.reshape(hidden // 128, 128), w_proj, near, t2i)
    far_expo, sums = call(
        far_kernel, "far", [((rows, half), F32), ((1, texts + 128), F32)], [smem] + [vmem] * 4, int(1e8)
    )(pos, proj, far, t2i, near_sums)
    swapped = swap(sums)
    row_loss, rowg, sums = call(
        rows_kernel,
        "rows",
        [((1, count), F32), ((rows, embed), F32), ((1, texts + 128), F32)],
        [smem] * 2 + [vmem] * 5,
        int(2e10),
    )(pos, i2t_index, near_expo, far_expo, near, far, sums)

    total = sums + swapped
    total = jnp.sum(spread(total, ("y_lo", "x", "y_hi"), sizes["y_lo"] * sizes["x"] * sizes["y_hi"]), axis=0)
    total = spread(total, "z", sizes["z"])

    query_grad, col_loss = call(
        grads_kernel,
        "grads",
        [((rows, hidden), BF16), ((1, block), F32)],
        [smem] + [vmem] * 9,
        int(2e8),
        [pltpu.VMEM((1, texts), F32)],
    )(pos, total, t2i, near_expo, far_expo, near, far, rowg, proj, w_proj)
    return (
        query_grad.reshape(count, queries, hidden),
        row_loss.reshape(count),
        col_loss.reshape(block),
    )


def solution(mesh):
    sizes = {"y_lo": 2, "x": mesh.shape["img"] // 2, "z": mesh.shape["txt"] // 4, "y_hi": 2, "core": 2}
    fine = Mesh(mesh.devices.reshape(tuple(sizes.values())), tuple(sizes))
    everywhere = tuple(sizes)
    text = ("z", "y_hi", "core")
    return jax.shard_map(
        functools.partial(local, sizes),
        mesh=fine,
        in_specs=(
            P(everywhere, None, None),
            P(),
            P(),
            P(),
            P(),
            P(),
            P(),
            P(),
            P(text, None),
            P(),
            P(),
        ),
        out_specs=(P(everywhere, None, None), P(everywhere), P(text)),
        check_vma=False,
    )
```

```python
import functools

import jax
import jax.numpy as jnp
from jax import lax
from jax.experimental import pallas as pl
from jax.experimental.pallas import tpu as pltpu
from jax.sharding import Mesh
from jax.sharding import PartitionSpec as P

HEAD = 64
LOGIT_SCALE = 1.0 / 0.07
GROUP = 4

BF16 = jnp.bfloat16
F32 = jnp.float32


def dot(a, b):
    return jnp.dot(a, b, preferred_element_type=F32)


def dot_nt(a, b):
    return lax.dot_general(a, b, (((1,), (1,)), ((), ())), preferred_element_type=F32)


def dot_tn(a, b):
    return lax.dot_general(a, b, (((0,), (0,)), ((), ())), preferred_element_type=F32)


def encode_kernel(
    count,
    block,
    feats_hbm,
    qs_hbm,
    wq_hbm,
    wk_hbm,
    wv_hbm,
    wo_hbm,
    t2i_ref,
    mixed_ref,
    turned_ref,
    feats_ref,
    qs_ref,
    wq_ref,
    wk_ref,
    wv_ref,
    flat_ref,
    qk_ref,
    values_ref,
    wo_ref,
    att_ref,
    sems,
):
    queries, hidden = qs_ref.shape
    patches, _, width = feats_ref.shape
    cols = GROUP * HEAD
    rows = GROUP * queries
    groups = hidden // cols
    total = patches * count
    texts = t2i_ref.shape[1]
    for k in range(texts // block):
        at = (k % 2) * (texts // 2) + k // 2 * block
        turned_ref[:, at : at + block] = t2i_ref[:, k * block : (k + 1) * block]
    row_head = lax.broadcasted_iota(jnp.int32, (rows, cols), 0) // queries
    col_head = lax.broadcasted_iota(jnp.int32, (rows, cols), 1) // HEAD
    own_head = row_head == col_head

    cut = patches // 2
    spans = (slice(0, cut), slice(cut, patches))
    pairs = (
        (qs_hbm, qs_ref),
        (wq_hbm, wq_ref),
        (wk_hbm, wk_ref),
        (feats_hbm.at[spans[0]], feats_ref.at[spans[0]]),
        (feats_hbm.at[spans[1]], feats_ref.at[spans[1]]),
        (wv_hbm, wv_ref),
        (wo_hbm, wo_ref),
    )
    copies = [pltpu.make_async_copy(s, d, sems.at[i]) for i, (s, d) in enumerate(pairs)]
    for c in copies:
        c.start()

    def project(p):
        lo, hi = p.start * count, p.stop * count
        flat_ref[lo:hi] = feats_ref[p].reshape(hi - lo, width)
        return lo, hi

    copies[0].wait()
    copies[1].wait()
    qhead = dot(qs_ref[...], wq_ref[...]).astype(BF16)
    copies[2].wait()
    for g in range(groups):
        piece = qhead[:, g * cols : (g + 1) * cols].astype(F32) * (HEAD**-0.5)
        tiled = jnp.concatenate([piece] * GROUP, axis=0)
        spread_out = jnp.where(own_head, tiled, 0.0).astype(BF16)
        qk_ref[:, g * rows : (g + 1) * rows] = dot_nt(wk_ref[:, g * cols : (g + 1) * cols], spread_out).astype(BF16)
    copies[3].wait()
    copies[4].wait()
    project(spans[0])
    project(spans[1])
    scores = dot(flat_ref[...], qk_ref[...])
    copies[5].wait()
    copies[6].wait()
    whole = total // 8 * 8
    body = scores[:whole].reshape(whole // 8, 8, groups * rows)
    tail = scores[whole:]
    peak8 = jnp.max(body, axis=0)
    peak = functools.reduce(jnp.maximum, [peak8[i : i + count] for i in range(0, 8, count)] + [tail])
    body = jnp.exp(body - jnp.concatenate([peak] * (8 // count), axis=0)[None])
    tail = jnp.exp(tail - peak)
    sum8 = jnp.sum(body, axis=0)
    norm = 1.0 / (sum(sum8[i : i + count] for i in range(0, 8, count)) + tail)
    norm = jnp.concatenate([norm] * (8 // count), axis=0)
    probs = body.reshape(whole, groups * rows).astype(BF16)
    tail = tail.astype(BF16).astype(F32)
    values_ref[...] = dot(flat_ref[...], wv_ref[...]).astype(BF16)
    owner = lax.broadcasted_iota(jnp.int32, (rows, whole), 1) % count
    owns = [(owner == b).astype(F32).astype(BF16) for b in range(count)]
    for g in range(groups):
        turned = probs[:, g * rows : (g + 1) * rows].T
        parts = [turned * owns[b] for b in range(count)]
        out = dot(jnp.concatenate(parts, axis=0), values_ref[:whole, g * cols : (g + 1) * cols])
        scale = norm[:, g * rows : (g + 1) * rows].T
        last = tail[:, g * rows : (g + 1) * rows].T
        ends = values_ref[whole:, g * cols : (g + 1) * cols].astype(F32)
        for b in range(count):
            own = out[b * rows : (b + 1) * rows] + last[:, b : b + 1] * ends[b : b + 1]
            own = jnp.where(own_head, own * scale[:, b : b + 1], 0.0)
            att = sum(own[h * queries : (h + 1) * queries] for h in range(GROUP))
            att_ref[b * queries : (b + 1) * queries, g * cols : (g + 1) * cols] = att.astype(BF16)
    states = qs_ref[...].astype(F32)
    mixed_ref[...] = dot(att_ref[...], wo_ref[...]) + jnp.concatenate([states] * count, axis=0)


def encode(block, feats, query_states, w_query, w_key, w_value, w_out, t2i_index):
    count, patches, width = feats.shape
    queries, hidden = query_states.shape
    texts = t2i_index.shape[0]
    hbm = pl.BlockSpec(memory_space=pltpu.HBM)
    vmem = pl.BlockSpec(memory_space=pltpu.VMEM)
    return pl.pallas_call(
        functools.partial(encode_kernel, count, block),
        out_shape=(
            jax.ShapeDtypeStruct((count * queries, hidden), F32),
            jax.ShapeDtypeStruct((1, texts), jnp.int32),
        ),
        in_specs=[hbm] * 6 + [vmem],
        out_specs=(vmem, vmem),
        scratch_shapes=[
            pltpu.VMEM((patches, count, width), BF16),
            pltpu.VMEM(query_states.shape, BF16),
            pltpu.VMEM(w_query.shape, BF16),
            pltpu.VMEM(w_key.shape, BF16),
            pltpu.VMEM(w_value.shape, BF16),
            pltpu.VMEM((patches * count, width), BF16),
            pltpu.VMEM((width, hidden // HEAD * queries), BF16),
            pltpu.VMEM((patches * count, hidden), BF16),
            pltpu.VMEM(w_out.shape, BF16),
            pltpu.VMEM((count * queries, hidden), BF16),
            pltpu.SemaphoreType.DMA((7,)),
        ],
        compiler_params=pltpu.CompilerParams(vmem_limit_bytes=52 * 2**20),
        cost_estimate=pl.CostEstimate(flops=int(5.5e9), bytes_accessed=int(1.1e7), transcendentals=int(5e5)),
        name="encode",
    )(
        jnp.transpose(feats, (1, 0, 2)),
        query_states,
        w_query,
        w_key,
        w_value,
        w_out,
        t2i_index.reshape(1, texts),
    )


def normed(proj):
    inverse = lax.rsqrt(jnp.sum(proj * proj, axis=-1, keepdims=True) + 1e-06)
    return proj * inverse, inverse


def normalise_kernel(raw_ref, copies_ref):
    raw = raw_ref[...].astype(F32)
    text = (raw * lax.rsqrt(jnp.sum(raw * raw, axis=-1, keepdims=True) + 1e-06)).astype(BF16)
    for k in range(copies_ref.shape[0]):
        copies_ref[k] = text


def half_range(core, half):
    return pl.ds(pl.multiple_of(core * half, half), half)


def masks(count, rows, half, pos_ref, core, t2i):
    row = lax.broadcasted_iota(jnp.int32, (rows, 1), 0)
    col = lax.broadcasted_iota(jnp.int32, (1, half), 1)
    queries = rows // count
    image = row // queries
    chosen = row - image * queries == t2i
    same = image + (pos_ref[1] - core * half) == col
    return image, chosen, same


def logits_of(proj_ref, text):
    unit = normed(proj_ref[...])[0].astype(BF16)
    return dot_nt(unit, text) * LOGIT_SCALE


def columns(count, pos_ref, core, proj_ref, text_ref, t2i_ref, expo_ref):
    rows = proj_ref.shape[0]
    half = text_ref.shape[0]
    scores = logits_of(proj_ref, text_ref[...])
    image, chosen, same = masks(count, rows, half, pos_ref, core, t2i_ref[:, half_range(core, half)])
    expo = jnp.exp(scores)
    expo_ref[...] = expo
    total = jnp.sum(jnp.where(chosen, expo, 0.0), axis=0, keepdims=True)
    diag = jnp.sum(jnp.where(chosen & same, scores, 0.0), axis=1, keepdims=True)
    lane = lax.broadcasted_iota(jnp.int32, (rows, 128), 1)
    diag = jnp.sum(jnp.where(lane == pos_ref[4] + image, diag, 0.0), axis=0, keepdims=True)
    return total, diag


def near_kernel(
    count,
    pos_ref,
    mixed_ref,
    gain_ref,
    wp_ref,
    text_ref,
    t2i_ref,
    proj_ref,
    expo_ref,
    sums_ref,
):
    hidden = mixed_ref.shape[1]
    mixed = mixed_ref[...]
    centered = mixed - jnp.mean(mixed, axis=-1, keepdims=True)
    variance = jnp.mean(centered * centered, axis=-1, keepdims=True)
    gain = jnp.concatenate([gain_ref[k : k + 1, :] for k in range(hidden // 128)], axis=1)
    q_out = centered * lax.rsqrt(variance + 1e-06) * gain
    proj_ref[...] = dot(q_out.astype(BF16), wp_ref[...])
    half = text_ref.shape[0]
    total, diag = columns(count, pos_ref, pos_ref[2], proj_ref, text_ref, t2i_ref, expo_ref)
    sums_ref[:, :half] = total
    sums_ref[:, half:] = diag


def far_kernel(count, pos_ref, proj_ref, text_ref, t2i_ref, near_ref, expo_ref, sums_ref):
    half = text_ref.shape[0]
    core = pos_ref[2]
    total, diag = columns(count, pos_ref, 1 - core, proj_ref, text_ref, t2i_ref, expo_ref)
    sums_ref[:, half_range(core, half)] = near_ref[:, :half]
    sums_ref[:, half_range(1 - core, half)] = total
    sums_ref[:, 2 * half :] = near_ref[:, half:] + diag


def rows_kernel(
    count, pos_ref, i2t_ref, near_expo_ref, far_expo_ref, near_ref, far_ref, sums_ref, row_loss_ref, rowg_ref, again_ref
):
    again_ref[...] = sums_ref[...]
    rows, half = near_expo_ref.shape
    queries = rows // count
    core = pos_ref[2]
    row = lax.broadcasted_iota(jnp.int32, (rows, 1), 0)
    picked = functools.reduce(
        jnp.logical_or, [row == b * queries + i2t_ref[pos_ref[0] + b] for b in range(count)]
    )
    sides = ((near_ref, near_expo_ref, core), (far_ref, far_expo_ref, 1 - core))
    row_total = sum(jnp.sum(expo[...], axis=1, keepdims=True) for _, expo, _ in sides)
    scale = 1.0 / row_total
    own = 0.0
    rowg = 0.0
    for text, expo, side in sides:
        image, _, same = masks(count, rows, half, pos_ref, side, 0)
        own = own + jnp.sum(jnp.where(same, expo[...], 0.0), axis=1, keepdims=True)
        g_row = jnp.where(picked, expo[...] * scale - same.astype(F32), 0.0)
        rowg = rowg + dot(g_row.astype(BF16), text[...])
    rowg_ref[...] = rowg
    row_loss = jnp.where(picked, jnp.log(row_total) - jnp.log(own), 0.0)
    lane = lax.broadcasted_iota(jnp.int32, (rows, 128), 1)
    row_loss = jnp.sum(jnp.where(lane == image, row_loss, 0.0), axis=0, keepdims=True)
    row_loss_ref[...] = row_loss[:, :count]


def grads_kernel(
    count,
    pos_ref,
    sums_ref,
    t2i_ref,
    near_expo_ref,
    far_expo_ref,
    near_ref,
    far_ref,
    rowg_ref,
    proj_ref,
    wp_ref,
    grad_ref,
    col_loss_ref,
    total_ref,
):
    rows, half = near_expo_ref.shape
    core = pos_ref[2]
    planes = sums_ref.shape[0]
    total = sum(sums_ref[k, :, : 2 * half] for k in range(planes))
    total_ref[...] = total
    block = col_loss_ref.shape[1]
    part = block // 2
    at = pos_ref[3] * block // part
    plane, slot = at % planes, at // planes * part
    first = jnp.broadcast_to(sums_ref[plane, :, 2 * half :], (8, 128))
    second = jnp.broadcast_to(sums_ref[plane + 1, :, 2 * half :], (8, 128))
    first = pltpu.roll(first, (128 - slot) % 128, 1)
    second = pltpu.roll(second, (128 - slot + part) % 128, 1)
    lane = lax.broadcasted_iota(jnp.int32, (8, 128), 1)
    diag = jnp.where(lane < part, first, second)
    start = core * half + pos_ref[3] // 2 * block
    lse = pltpu.roll(jnp.broadcast_to(jnp.log(total), (8, 2 * half)), (2 * half - start) % (2 * half), 1)
    col_loss_ref[...] = lse[0:1, :block] - diag[0:1, :block]

    grad = rowg_ref[...]
    for text, expo, side in ((near_ref, near_expo_ref, core), (far_ref, far_expo_ref, 1 - core)):
        span = half_range(side, half)
        _, chosen, same = masks(count, rows, half, pos_ref, side, t2i_ref[:, span])
        g_col = jnp.where(chosen, expo[...] * (1.0 / total_ref[:, span]) - same.astype(F32), 0.0)
        grad = grad + dot(g_col.astype(BF16), text[...])
    g_emb = LOGIT_SCALE * grad
    unit, inverse = normed(proj_ref[...])
    g_proj = inverse * (g_emb - unit * jnp.sum(unit * g_emb, axis=-1, keepdims=True))
    grad_ref[...] = dot_nt(g_proj.astype(BF16), wp_ref[...]).astype(BF16)


def spread(x, axes, n):
    return lax.all_to_all(jnp.broadcast_to(x[None], (n,) + x.shape), axes, 0, 0, tiled=True)


def text_groups(sizes):
    z, hi = sizes["z"], sizes["y_hi"]
    return [[((side ^ h) * z + k) * hi + h for k in range(z) for h in range(hi)] for side in range(hi)]


def swap(x):
    return lax.ppermute(x, "core", [(0, 1), (1, 0)])


def local(
    sizes,
    feats,
    query_states,
    w_query,
    w_key,
    w_value,
    w_out,
    ln_gain,
    w_proj,
    text_feats,
    i2t_index,
    t2i_index,
):
    count = feats.shape[0]
    queries, hidden = query_states.shape
    embed = w_proj.shape[1]
    block = text_feats.shape[0]
    rows = count * queries
    texts = t2i_index.shape[0]
    half = texts // 2
    txt = lax.axis_index(("z", "y_hi", "core"))
    img = lax.axis_index(("y_lo", "x"))
    core = lax.axis_index("core")
    first = (img * (texts // block) + txt) * count
    home = first // block
    place = home % 2 * half + home // 2 * block + first % block
    slot = img * (sizes["y_hi"] * sizes["core"]) + lax.axis_index("y_hi") * sizes["core"] + core
    pos = jnp.stack([first, place, core, txt, slot * count]).astype(jnp.int32)

    vmem = pl.BlockSpec(memory_space=pltpu.VMEM)
    smem = pl.BlockSpec(memory_space=pltpu.SMEM)
    near_count = sizes["z"] * sizes["y_hi"]
    copies = pl.pallas_call(
        normalise_kernel,
        out_shape=jax.ShapeDtypeStruct((near_count,) + text_feats.shape, BF16),
        in_specs=[vmem],
        out_specs=vmem,
        compiler_params=pltpu.CompilerParams(vmem_limit_bytes=2 * 2**20),
        cost_estimate=pl.CostEstimate(flops=int(2e10), bytes_accessed=int(6e7), transcendentals=0),
        name="normalise",
    )(text_feats)
    near = lax.all_to_all(
        copies, ("y_lo", "z", "y_hi"), 0, 0, axis_index_groups=text_groups(sizes), tiled=True
    ).reshape(half, embed)
    mixed, t2i = encode(block, feats, query_states, w_query, w_key, w_value, w_out, t2i_index)
    far = swap(near)

    def call(kernel, name, outs, specs, flops, scratch=()):
        return pl.pallas_call(
            functools.partial(kernel, count),
            out_shape=tuple(jax.ShapeDtypeStruct(*o) for o in outs),
            in_specs=specs,
            out_specs=(vmem,) * len(outs),
            scratch_shapes=scratch,
            compiler_params=pltpu.CompilerParams(vmem_limit_bytes=16 * 2**20),
            cost_estimate=pl.CostEstimate(flops=flops, bytes_accessed=int(2e6), transcendentals=rows * texts),
            name=name,
        )

    proj, near_expo, near_sums = call(
        near_kernel,
        "near",
        [((rows, embed), F32), ((rows, half), F32), ((1, half + 128), F32)],
        [smem] + [vmem] * 5,
        int(2e10),
    )(pos, mixed, ln_gain.reshape(hidden // 128, 128), w_proj, near, t2i)
    far_expo, sums = call(
        far_kernel, "far", [((rows, half), F32), ((1, texts + 128), F32)], [smem] + [vmem] * 4, int(1e8)
    )(pos, proj, far, t2i, near_sums)
    swapped = swap(sums)
    row_loss, rowg, sums = call(
        rows_kernel,
        "rows",
        [((1, count), F32), ((rows, embed), F32), ((1, texts + 128), F32)],
        [smem] * 2 + [vmem] * 5,
        int(2e10),
    )(pos, i2t_index, near_expo, far_expo, near, far, sums)

    total = sums + swapped
    total = jnp.sum(spread(total, ("y_lo", "x", "y_hi"), sizes["y_lo"] * sizes["x"] * sizes["y_hi"]), axis=0)
    total = spread(total, "z", sizes["z"])

    query_grad, col_loss = call(
        grads_kernel,
        "grads",
        [((rows, hidden), BF16), ((1, block), F32)],
        [smem] + [vmem] * 9,
        int(2e8),
        [pltpu.VMEM((1, texts), F32)],
    )(pos, total, t2i, near_expo, far_expo, near, far, rowg, proj, w_proj)
    return (
        query_grad.reshape(count, queries, hidden),
        row_loss.reshape(count),
        col_loss.reshape(block),
    )


def solution(mesh):
    sizes = {"y_lo": 2, "x": mesh.shape["img"] // 2, "z": mesh.shape["txt"] // 4, "y_hi": 2, "core": 2}
    fine = Mesh(mesh.devices.reshape(tuple(sizes.values())), tuple(sizes))
    everywhere = tuple(sizes)
    text = ("z", "y_hi", "core")
    return jax.shard_map(
        functools.partial(local, sizes),
        mesh=fine,
        in_specs=(
            P(everywhere, None, None),
            P(),
            P(),
            P(),
            P(),
            P(),
            P(),
            P(),
            P(text, None),
            P(),
            P(),
        ),
        out_specs=(P(everywhere, None, None), P(everywhere), P(text)),
        check_vma=False,
    )
```
